256 devices in a mesh: lat: 64 (over x, z, y_hi), lon: 4 (over y_lo, core).
Axes of the slice: x: 4, y: 4 (y_hi: 2, y_lo: 2; y = y_hi * 2 + y_lo), z: 8, core: 2. Of those that a mesh axis runs over, the one named last changes fastest.
Arguments:
- state: bfloat16 [76, 768, 1080], P(None, 'lat', 'lon'), may hold values from -6 to 6
- sea_mask: int32 [19, 768, 1080], P(None, 'lat', 'lon'), may hold values 0 or 1
- seam: int32 [1080], replicated, may hold values from 0 to 1079, as said below
- w_in: bfloat16 [3, 3, 200, 76], replicated, may hold values from -0.21875 to 0.21875
- w_down: bfloat16 [2, 2, 200, 200], replicated, may hold values from -0.21875 to 0.21875
- w_mid: bfloat16 [3, 3, 200, 200], replicated, may hold values from -0.125 to 0.125
- w_up: bfloat16 [2, 2, 200, 200], replicated, may hold values from -0.4375 to 0.4375
- w_out: bfloat16 [3, 3, 76, 200], replicated, may hold values from -0.125 to 0.125
Outputs:
- next_state: bfloat16 [76, 768, 1080], P(None, 'lat', 'lon')
The draws below stay inside these ranges and needn't reach their ends.
Inputs may be any that keep to these rules, and one draw needn't show every extreme that they name: The fold is a mirror: seam[j] = (c - j) mod 1080 for one odd c, the same for all j, drawn from the seed; so longitudes 2 k and 2 k + 1 name 2 m + 1 and 2 m for one m, and seam[seam[j]] = j.
All inputs are finite; a program needn't handle non-finite values. No bound on the sum of `sea_mask` on one device may be relied on, other than what follows from the above.
Results may differ from the reference program's by a relative error of at most 0.004.
Values may be sent and summed in bfloat16 or wider, within the bound.
No kernel may reach another device: no remote copies, remote signals or barrier semaphores. Data moves between devices by JAX's collectives and lax.ppermute only.
A program may use at most 64 MiB of HBM per device.

```python
import jax
import jax.numpy as jnp
from jax import lax

VARS = 4
LEVELS = 19
CHANNELS = 76
HIDDEN_SIZE = 200
ROWS_DEV = 12
LATS = 768
LONS = 1080
N_LAT = 64


def draw_seam(key, part):
    key = jax.random.fold_in(key, 7)
    offset = 2 * jax.random.randint(key, (), 0, LONS // 2).astype(jnp.int32) + 1
    columns = jnp.arange(LONS, dtype=jnp.int32)
    return jnp.mod(offset - columns, LONS).astype(jnp.int32)


def with_ends(values, stream_key, smallest, largest):
    longest = values.shape.index(max(values.shape))
    spots = []
    for shift in (0, 1):
        where = [jax.random.randint(jax.random.fold_in(stream_key, axis), (), 0, length) for axis, length in enumerate(values.shape)]
        where[longest] = (where[longest] + shift) % values.shape[longest]
        spots.append(tuple(where))
    return values.at[spots[0]].set(smallest).at[spots[1]].set(largest)


def steps_of(own_key, dims, shards, smallest, top_value):
    factor_of = 1.0
    for dim, shards_of in shards:
        heights = jax.random.uniform(jax.random.fold_in(jax.random.fold_in(own_key, 6), dim), (shards_of,), jnp.float32, smallest / len(shards), top_value / len(shards))
        factor_of = factor_of * jnp.repeat(jnp.exp(heights), dims[dim] // shards_of).reshape((-1,) + (1,) * (len(dims) - 1 - dim))
    return factor_of


def scatter_about(rng, extent, scale, most, shards=(), held_as=jnp.bfloat16):
    array = jax.random.normal(rng, extent, jnp.float32) * scale
    if len(shards) > 0:
        array = steps_of(rng, extent, shards, -0.22, 0.18) * array
    return jnp.clip(array, min=-most, max=most).astype(held_as)


def setup_inputs(seed: int = 0) -> dict:
    streams_of = jax.random.split(jax.random.key(seed), 9)
    return {
        "state": scatter_about(streams_of[0], (CHANNELS, LATS, LONS), 1.0, 6.0, ((1, 64), (2, 4))),
        "sea_mask": with_ends((jax.random.randint(streams_of[1], (LEVELS, LATS, LONS), 0, 4) < 3).astype(jnp.int32), jax.random.fold_in(streams_of[1], 1), 0, 1),
        "seam": draw_seam(jax.random.fold_in(streams_of[8], 71), 0),
        "w_in": scatter_about(streams_of[3], (3, 3, HIDDEN_SIZE, CHANNELS), (9 * CHANNELS) ** -0.5, 0.21875),
        "w_down": scatter_about(streams_of[4], (2, 2, HIDDEN_SIZE, HIDDEN_SIZE), (4 * HIDDEN_SIZE) ** -0.5, 0.21875),
        "w_mid": scatter_about(streams_of[5], (3, 3, HIDDEN_SIZE, HIDDEN_SIZE), (9 * HIDDEN_SIZE) ** -0.5, 0.125),
        "w_up": scatter_about(streams_of[6], (2, 2, HIDDEN_SIZE, HIDDEN_SIZE), HIDDEN_SIZE ** -0.5, 0.4375),
        "w_out": scatter_about(streams_of[7], (3, 3, CHANNELS, HIDDEN_SIZE), (9 * HIDDEN_SIZE) ** -0.5, 0.125),
    }


def extend(field, seam_map):
    fold = jnp.take(field[:, -1, :], seam_map, axis=1)[:, None, :]
    rows = jnp.concatenate([jnp.zeros_like(field[:, :1, :]), field, fold], axis=1)
    return jnp.concatenate([rows[:, :, -1:], rows, rows[:, :, :1]], axis=2)


def conv_band(extended, weight, start, count):
    width = extended.shape[2] - 2
    piece = lax.dynamic_slice_in_dim(extended, start, count + 2, 1).astype(jnp.float32)
    total = jnp.zeros((weight.shape[2], count, width), jnp.float32)
    for row_tap in range(3):
        for col_tap in range(3):
            total = total + jnp.einsum("oc,crl->orl", weight[row_tap, col_tap].astype(jnp.float32), piece[:, row_tap:row_tap + count, col_tap:col_tap + width])
    return total


def by_bands(func):
    stacked = lax.map(func, jnp.arange(N_LAT, dtype=jnp.int32))
    return jnp.moveaxis(stacked, 0, 1).reshape(stacked.shape[1], -1, stacked.shape[3])


def reference(state, sea_mask, seam, w_in, w_down, w_mid, w_up, w_out):
    rows = ROWS_DEV
    half = rows // 2
    cover = jnp.tile(sea_mask, (VARS, 1, 1)).astype(jnp.float32)
    masked = (state.astype(jnp.float32) * cover).astype(jnp.bfloat16)
    ext_first = extend(masked, seam)
    first = by_bands(lambda band: jax.nn.gelu(conv_band(ext_first, w_in, band * rows, rows), approximate=True).astype(jnp.bfloat16))

    def down(band):
        piece = lax.dynamic_slice_in_dim(first, band * rows, rows, 1).astype(jnp.float32)
        piece = piece.reshape(HIDDEN_SIZE, half, 2, LONS // 2, 2)
        return jax.nn.gelu(jnp.einsum("abxc,ciajb->xij", w_down.astype(jnp.float32), piece), approximate=True).astype(jnp.bfloat16)

    coarse = by_bands(down)
    ext_coarse = extend(coarse, seam[0::2] // 2)
    middle = by_bands(lambda band: jax.nn.gelu(conv_band(ext_coarse, w_mid, band * half, half), approximate=True).astype(jnp.bfloat16))

    def up(band):
        piece = lax.dynamic_slice_in_dim(middle, band * half, half, 1).astype(jnp.float32)
        grown = jnp.einsum("abxc,cij->xiajb", w_up.astype(jnp.float32), piece).reshape(HIDDEN_SIZE, rows, LONS)
        skip = lax.dynamic_slice_in_dim(first, band * rows, rows, 1).astype(jnp.float32)
        return (jax.nn.gelu(grown, approximate=True) + skip).astype(jnp.bfloat16)

    joined = by_bands(up)
    ext_joined = extend(joined, seam)

    def finish(band):
        delta = conv_band(ext_joined, w_out, band * rows, rows)
        base = lax.dynamic_slice_in_dim(state, band * rows, rows, 1).astype(jnp.float32)
        keep = lax.dynamic_slice_in_dim(cover, band * rows, rows, 1)
        return ((base + delta) * keep).astype(jnp.bfloat16)

    return by_bands(finish)
```

```python
import jax
import jax.numpy as jnp
from jax import lax
from jax.experimental import pallas as pl
from jax.experimental.pallas import tpu as pltpu
from jax.sharding import PartitionSpec as P

VARS, LEVELS, CHANNELS, HIDDEN = 4, 19, 76, 200
ROWS, COLS = 12, 270
HALO = 5
CH = 80
LANES = 384
MAIN = 256
REST = COLS - MAIN
PIX = 144
HID = 256
TROWS = 408
F32, BF16 = jnp.float32, jnp.bfloat16


def gelu(x):
    inner = x * (0.7978845608028654 + 0.035677408136300125 * (x * x))
    half = 0.5 * x
    return half + half * jnp.tanh(inner)


def prep_kernel(state_ref, mask_ref, rows_ref, lon_ref, north_ref, south_ref, wide_ref):
    for t in range(3):
        wide_ref[t, CHANNELS:] = jnp.zeros((CH - CHANNELS, 16, 128), F32)

    def level(l, carry):
        cover = mask_ref[l].astype(F32)
        for v in range(VARS):
            masked = state_ref[v * LEVELS + l].astype(F32) * cover
            masked = jnp.concatenate([masked, jnp.zeros((ROWS, LANES - COLS), F32)], axis=1)
            for t in range(3):
                wide_ref[t, v * LEVELS + l, 0:ROWS] = masked[:, t * 128 : (t + 1) * 128]
        return carry

    lax.fori_loop(0, LEVELS, level, 0)
    flat = wide_ref.reshape(3 * CH * 16, 128)
    at = lambda r: [flat[pl.ds(t * CH * 16 + r, CH, stride=16), :] for t in range(3)]
    rows = [jnp.concatenate(at(r), axis=1) for r in range(ROWS)]
    for r in range(ROWS):
        rows_ref[r] = rows[r].astype(BF16)
    zeros = lambda n: [jnp.zeros((CH, n), F32)]
    low = jnp.concatenate([row[:, :HALO] for row in rows] + zeros(128 - ROWS * HALO), axis=1)
    high = jnp.concatenate([row[:, COLS - HALO : COLS] for row in rows] + zeros(128 - ROWS * HALO), axis=1)
    lon_ref[0] = low.astype(BF16)
    lon_ref[1] = high.astype(BF16)
    for ref, first in ((north_ref, ROWS - HALO), (south_ref, 0)):
        picked = rows[first : first + HALO]
        for k in range(HALO):
            ref[k * CH : (k + 1) * CH, :] = picked[k][:, :MAIN].astype(BF16)
        tail = jnp.concatenate([row[:, MAIN:COLS] for row in picked] + zeros(128 - HALO * REST), axis=1).astype(BF16)
        ref[HALO * CH :, :] = jnp.concatenate([tail[: CH // 2], tail[CH // 2 :]], axis=1)


def prep(state, mask):
    vmem = pl.BlockSpec(memory_space=pltpu.VMEM)
    payload = jax.ShapeDtypeStruct((HALO * CH + CH // 2, MAIN), BF16)
    return pl.pallas_call(
        prep_kernel,
        out_shape=(
            jax.ShapeDtypeStruct((ROWS, CH, LANES), BF16),
            jax.ShapeDtypeStruct((2, CH, 128), BF16),
            payload,
            payload,
        ),
        in_specs=[vmem] * 2,
        out_specs=(vmem,) * 4,
        scratch_shapes=[pltpu.VMEM((3, CH, 16, 128), F32)],
        compiler_params=pltpu.CompilerParams(vmem_limit_bytes=40 * 2**20),
    )(state, mask)


def tail_of(payload_ref):
    low = payload_ref[HALO * CH :, :]
    return jnp.concatenate([low[:, :128], low[:, 128:]], axis=0).astype(F32)


def flip(block):
    n = block.shape[1]
    return jnp.concatenate([block, jnp.zeros((128 - CH, n), F32)], axis=0).T


def main_kernel(
    seam_ref, rows_ref, west_ref, east_ref, south_ref, north_ref, fold1_ref, fold2_ref, fold3_ref, own_ref,
    w_in_ref, w_down_ref, w_mid_ref, w_up_ref, w_out_ref, state_ref, mask_ref,
    out_ref,
    t_ref, edge_ref, a_ref, f_ref, c_ref, j_ref, u_ref, y_ref, d_ref,
):
    n_lat, n_lon = lax.axis_size("lat"), lax.axis_size("lon")
    lat, lon = lax.axis_index("lat"), lax.axis_index("lon")
    bottom, top = lat == 0, lat == n_lat - 1
    keep = jnp.where(bottom, 0.0, 1.0).astype(F32)

    lane = lax.broadcasted_iota(jnp.int32, (PIX, 128), 1)

    def pack(ai):
        odd_left, even, odd, even_right = (t_ref[pl.ds(3 + s, PIX, stride=2), :] for s in range(4))
        even80, odd80 = pltpu.roll(even, CH, 1), pltpu.roll(odd, CH, 1)
        for p, (left, mid, right) in enumerate(((odd_left, even80, odd), (even, odd80, even_right))):
            low = jnp.where(lane < CH, left, mid)
            high = jnp.where(lane < 2 * CH - 128, mid, pltpu.roll(right, 2 * CH - 128, 1))
            a_ref[ai, p * PIX : (p + 1) * PIX, :] = jnp.concatenate([low, high], axis=1).astype(BF16)

    edge_ref[0] = flip(west_ref[...].astype(F32))
    edge_ref[1] = flip(east_ref[...].astype(F32))
    edge_ref[2] = flip(tail_of(south_ref))
    edge_ref[3] = flip(tail_of(north_ref))

    def own_row(r, carry):
        t_ref[8 : 8 + LANES, :] = flip(rows_ref[r].astype(F32))
        t_ref[8 - HALO : 8, :] = edge_ref[0, pl.ds(r * HALO, HALO), :]
        t_ref[8 + COLS : 8 + COLS + HALO, :] = edge_ref[1, pl.ds(r * HALO, HALO), :]
        pack(r + HALO)
        return carry

    lax.fori_loop(0, ROWS, own_row, 0)

    def halo_row(ref, side, k, ai):
        t_ref[8 : 8 + MAIN, :] = flip(ref[pl.ds(pl.multiple_of(k * CH, CH), CH), :].astype(F32))
        t_ref[8 + MAIN : 8 + COLS, :] = edge_ref[side, pl.ds(k * REST, REST), :]
        t_ref[8 - HALO : 8, :] = edge_ref[side, pl.ds(HALO * REST + k * HALO, HALO), :]
        t_ref[8 + COLS : 8 + COLS + HALO, :] = edge_ref[side, pl.ds(HALO * (REST + HALO) + k * HALO, HALO), :]
        pack(ai)

    def south_row(k, carry):
        @pl.when(bottom)
        def _():
            a_ref[k] = jnp.zeros((2 * PIX, HID), BF16)

        @pl.when(jnp.logical_not(bottom))
        def _():
            halo_row(south_ref, 2, k, k)

        return carry

    lax.fori_loop(0, HALO, south_row, 0)

    @pl.when(jnp.logical_not(top))
    def _():
        def north_row(k, carry):
            halo_row(north_ref, 3, k, ROWS + HALO + k)
            return carry

        lax.fori_loop(0, HALO, north_row, 0)

    @pl.when(top)
    def _():
        circle = n_lon * COLS
        span = 288
        column = lax.broadcasted_iota(jnp.int32, (span, 128), 0) - 8 + COLS * lon
        source = lax.rem(seam_ref[0] - column + 3 * circle, circle)
        spot = lax.broadcasted_iota(jnp.int32, (span, 128), 1)

        def fold_row(k, carry):
            kk = HALO - 1 - k
            total = jnp.zeros((span, CH), F32)
            for d, ref in enumerate((own_ref, fold1_ref, fold2_ref, fold3_ref)):
                block = lax.rem(lon + n_lon - d, n_lon)
                place = source - block * COLS
                hot = [(place == spot), (place == spot + 128)]
                inside = jnp.logical_and(place >= MAIN, place < COLS)
                hot.append(jnp.logical_and(inside, place - MAIN + kk * REST == spot))
                hot = jnp.concatenate([jnp.where(h, 1.0, 0.0).astype(BF16) for h in hot], axis=1)
                main = ref[pl.ds(pl.multiple_of(kk * CH, CH), CH), :]
                values = jnp.concatenate([main, tail_of(ref).astype(BF16)], axis=1)
                total += lax.dot_general(hot, values, (((1,), (1,)), ((), ())), preferred_element_type=F32)
            t_ref[0:span, :] = jnp.concatenate([total, jnp.zeros((span, 128 - CH), F32)], axis=1)
            pack(ROWS + HALO + k)
            return carry

        lax.fori_loop(0, HALO, fold_row, 0)

    def first_group(g, carry):
        turned = jnp.logical_and(top, g == 4)
        tap = lambda t, n: jnp.where(turned, n - 1 - t, t)
        w_in = [
            jnp.concatenate(
                [w_in_ref[tap(3 * a + b, 9)] for b in range(3)] + [jnp.zeros((HID - 3 * CH, HID), BF16)], axis=0
            )
            for a in range(3)
        ]
        w_in = jnp.concatenate(w_in, axis=0)
        for q in range(4):
            fr = 4 * g + q
            taps = jnp.concatenate([a_ref[fr + a] for a in range(3)], axis=1)
            f_ref[fr] = gelu(jnp.dot(taps, w_in, preferred_element_type=F32)).astype(BF16)
        w_down = jnp.concatenate([w_down_ref[tap(t, 4)] for t in range(4)], axis=0)
        for q in range(2):
            ci = 2 * g + q
            pieces = [f_ref[2 * ci + a, b * PIX : (b + 1) * PIX, :] for a in range(2) for b in range(2)]
            coarse = gelu(jnp.dot(jnp.concatenate(pieces, axis=1), w_down, preferred_element_type=F32))
            coarse = coarse * jnp.where(ci < 2, keep, 1.0)
            planes = [pltpu.roll(coarse, 1, 0), coarse, pltpu.roll(coarse, PIX - 1, 0)]
            c_ref[ci] = jnp.concatenate(planes, axis=1).astype(BF16)
        return carry

    lax.fori_loop(0, 5, first_group, 0)

    def mid_row(mi, carry):
        turned = jnp.logical_and(top, mi == 7)
        tap = lambda t, n: jnp.where(turned, n - 1 - t, t)
        taps = jnp.concatenate([c_ref[mi + a] for a in range(3)], axis=1)
        w_mid = jnp.concatenate([w_mid_ref[tap(t, 9)] for t in range(9)], axis=0)
        middle = gelu(jnp.dot(taps, w_mid, preferred_element_type=F32)).astype(BF16)
        held = jnp.where(mi < 1, keep, 1.0)
        for a in range(2):
            halves = []
            for b in range(2):
                grown = jnp.dot(middle, w_up_ref[tap(2 * a + b, 4)], preferred_element_type=F32)
                first = f_ref[2 * mi + a + 2, b * PIX : (b + 1) * PIX, :].astype(F32)
                halves.append((gelu(grown) + first) * held)
            even, odd = halves
            planes = (pltpu.roll(odd, 1, 0), even, odd, pltpu.roll(even, PIX - 1, 0))
            for s, plane in enumerate(planes):
                j_ref[2 * mi + a, s * PIX : (s + 1) * PIX, :] = plane.astype(BF16)
        return carry

    lax.fori_loop(0, 8, mid_row, 0)

    def out_part(i, carry):
        jr = i + 1
        taps = jnp.concatenate([j_ref[jr, b * PIX : (b + 2) * PIX, :] for b in range(3)], axis=1)
        part = jnp.dot(taps, w_out_ref[...], preferred_element_type=F32)
        for t in range(2):
            for p in range(2):
                half = part[p * PIX : (p + 1) * PIX, t * 128 : (t + 1) * 128]
                u_ref[pl.ds(t * TROWS + 4 + p, PIX, stride=2), :] = half
            y_ref[i, t * 128 : (t + 1) * 128, :] = u_ref[t * TROWS + 8 : t * TROWS + 8 + LANES, :].T
        return carry

    lax.fori_loop(0, ROWS + 2, out_part, 0)
    flat = d_ref.reshape(3 * CH * 16, 128)

    def out_row(r, carry):
        parts = [y_ref[r + a, a * CH : (a + 1) * CH, :] for a in range(3)]
        total = parts[0] + parts[1] + parts[2]
        for t in range(3):
            flat[pl.ds(t * CH * 16 + r, CH, stride=16), :] = total[:, t * 128 : (t + 1) * 128]
        return carry

    lax.fori_loop(0, ROWS, out_row, 0)

    def level(l, carry):
        cover = mask_ref[l].astype(F32)
        for v in range(VARS):
            c = v * LEVELS + l
            delta = jnp.concatenate([d_ref[t, c, 0:ROWS, :] for t in range(3)], axis=1)[:, :COLS]
            total = (state_ref[c].astype(F32) + delta) * cover
            out_ref[c] = total.astype(BF16)
        return carry

    lax.fori_loop(0, LEVELS, level, 0)


def main(*operands):
    vmem = pl.BlockSpec(memory_space=pltpu.VMEM)
    smem = pl.BlockSpec(memory_space=pltpu.SMEM)
    return pl.pallas_call(
        main_kernel,
        out_shape=jax.ShapeDtypeStruct((CHANNELS, ROWS, COLS), BF16),
        in_specs=[smem] + [vmem] * (len(operands) - 1),
        out_specs=vmem,
        scratch_shapes=[
            pltpu.VMEM((TROWS, 128), F32),
            pltpu.VMEM((4, 128, 128), F32),
            pltpu.VMEM((ROWS + 2 * HALO, 2 * PIX, HID), BF16),
            pltpu.VMEM((20, 2 * PIX, HID), BF16),
            pltpu.VMEM((10, PIX, 3 * HID), BF16),
            pltpu.VMEM((16, 4 * PIX, HID), BF16),
            pltpu.VMEM((2 * TROWS, 128), F32),
            pltpu.VMEM((ROWS + 2, HID, LANES), F32),
            pltpu.VMEM((3, CH, 16, 128), F32),
        ],
        compiler_params=pltpu.CompilerParams(vmem_limit_bytes=60 * 2**20),
    )(*operands)


def weights(w_in, w_down, w_mid, w_up, w_out):
    def laid(w, rows):
        w = jnp.swapaxes(w.reshape((-1,) + w.shape[2:]), 1, 2)
        return jnp.pad(w, ((0, 0), (0, rows - w.shape[1]), (0, HID - w.shape[2])))

    out = jnp.transpose(w_out, (1, 3, 0, 2))
    out = jnp.pad(out, ((0, 0), (0, HID - HIDDEN), (0, 0), (0, CH - CHANNELS))).reshape(3 * HID, 3 * CH)
    out = jnp.pad(out, ((0, 0), (0, HID - 3 * CH)))
    return laid(w_in, CH), laid(w_down, HID), laid(w_mid, HID), laid(w_up, HID), out


def body(state, sea_mask, seam, w_in, w_down, w_mid, w_up, w_out):
    n_lat, n_lon = lax.axis_size("lat"), lax.axis_size("lon")
    ring = lambda n, d: [(i, (i + d) % n) for i in range(n)]
    rows, edges, north_going, south_going = prep(state, sea_mask)
    west = lax.ppermute(edges[1], "lon", ring(n_lon, 1))
    east = lax.ppermute(edges[0], "lon", ring(n_lon, -1))

    def with_corners(payload, first):
        begin = HALO * REST
        pieces = []
        for side, edge in enumerate((west, east)):
            at = begin + side * HALO * HALO
            cut = edge[:, first * HALO : (first + HALO) * HALO]
            pieces.append(jnp.pad(cut, ((0, 0), (at, 128 - at - HALO * HALO))))
        added = pieces[0] + pieces[1]
        added = jnp.concatenate([added[: CH // 2], added[CH // 2 :]], axis=1)
        return payload.at[HALO * CH :].add(added)

    north_going = with_corners(north_going, ROWS - HALO)
    south_going = with_corners(south_going, 0)
    south = lax.ppermute(north_going, "lat", ring(n_lat, 1))
    north = lax.ppermute(south_going, "lat", ring(n_lat, -1))
    last = (n_lat - 1) * n_lon
    folds = [
        lax.ppermute(
            north_going,
            ("lat", "lon"),
            [(i, i) for i in range(last)] + [(last + j, last + (j + d) % n_lon) for j in range(n_lon)],
        )
        for d in (1, 2, 3)
    ]
    laid = weights(w_in, w_down, w_mid, w_up, w_out)
    return main(seam, rows, west, east, south, north, *folds, north_going, *laid, state, sea_mask)


def solution(mesh):
    return jax.shard_map(
        body,
        mesh=mesh,
        in_specs=(P(None, "lat", "lon"), P(None, "lat", "lon"), P(), P(), P(), P(), P(), P()),
        out_specs=P(None, "lat", "lon"),
        check_vma=False,
    )
```

```python
import jax
import jax.numpy as jnp
from jax import lax
from jax.experimental import pallas as pl
from jax.experimental.pallas import tpu as pltpu
from jax.sharding import PartitionSpec as P

VARS, LEVELS, CHANNELS, HIDDEN = 4, 19, 76, 200
ROWS, COLS = 12, 270
HALO = 5
CH = 80
LANES = 384
MAIN = 256
REST = COLS - MAIN
PAYLOAD = (HALO * CH + CH // 2, MAIN)
PIX = 144
HID = 256
TROWS = 408
CHUNK = 3
F32, BF16 = jnp.float32, jnp.bfloat16
VMEM = pl.BlockSpec(memory_space=pltpu.VMEM)
HBM = pl.BlockSpec(memory_space=pltpu.HBM)
SMEM = pl.BlockSpec(memory_space=pltpu.SMEM)


def dot_nt(a, b):
    return lax.dot_general(a, b, (((1,), (1,)), ((), ())), preferred_element_type=F32)


def gelu(x):
    inner = x * (0.7978845608028654 + 0.035677408136300125 * (x * x))
    half = 0.5 * x
    return half + half * jnp.tanh(inner)


def cost(us):
    return pl.CostEstimate(flops=int(us * 1e9), bytes_accessed=int(us * 3e6), transcendentals=0)


def call(kernel, ins, operands, outs, scratch, us, mib):
    return pl.pallas_call(
        kernel,
        out_shape=tuple(jax.ShapeDtypeStruct(shape, BF16) for shape in outs),
        in_specs=ins,
        out_specs=(VMEM,) * len(outs),
        scratch_shapes=scratch,
        cost_estimate=cost(us),
        compiler_params=pltpu.CompilerParams(vmem_limit_bytes=mib * 2**20),
    )(*operands)


def masked_row(state_ref, mask_ref, r):
    cover = mask_ref[r].astype(F32)
    row = state_ref[r].astype(F32) * jnp.concatenate([cover] * VARS, axis=0)
    row = jnp.concatenate([row, jnp.zeros((CHANNELS, LANES - COLS), F32)], axis=1)
    return jnp.concatenate([row, jnp.zeros((CH - CHANNELS, LANES), F32)], axis=0)


def tail_out(tail):
    return jnp.concatenate([tail[: CH // 2], tail[CH // 2 :]], axis=1).astype(BF16)


def tail_in(payload_ref):
    low = payload_ref[HALO * CH :, :]
    return jnp.concatenate([low[:, :128], low[:, 128:]], axis=0).astype(F32)


def edge_kernel(state_hbm, mask_hbm, rows_ref, east_ref, west_ref, fold_ref, state_ref, mask_ref, sems):
    copies = []
    for i in range(ROWS // CHUNK):
        rows = pl.ds(i * CHUNK, CHUNK)
        for j, (hbm, ref) in enumerate(((mask_hbm, mask_ref), (state_hbm, state_ref))):
            copies.append(pltpu.make_async_copy(hbm.at[rows], ref.at[rows], sems.at[j, i]))
            copies[-1].start()
    low, high, rest = [], [], []
    for r in range(ROWS):
        if r % CHUNK == 0:
            for copy in copies[2 * (r // CHUNK) : 2 * (r // CHUNK) + 2]:
                copy.wait()
        row = masked_row(state_ref, mask_ref, r)
        rows_ref[r] = row.astype(BF16)
        low.append(row[:, :HALO])
        high.append(row[:, COLS - HALO : COLS])
        k = r - (ROWS - HALO)
        if k >= 0:
            fold_ref[k * CH : (k + 1) * CH, :] = row[:, :MAIN].astype(BF16)
            rest.append(row[:, MAIN:COLS])
    zeros = lambda n: [jnp.zeros((CH, 128 - n), F32)]
    west_ref[...] = jnp.concatenate(low + zeros(ROWS * HALO), axis=1).astype(BF16)
    east_ref[...] = jnp.concatenate(high + zeros(ROWS * HALO), axis=1).astype(BF16)
    fold_ref[HALO * CH :, :] = tail_out(jnp.concatenate(rest + zeros(HALO * REST), axis=1))


def payload_kernel(rows_ref, west_ref, east_ref, pay0_ref, pay1_ref):
    odd = lax.rem(lax.axis_index("lat"), 2)
    lane = lax.broadcasted_iota(jnp.int32, (CH, 128), 1)
    beyond = []
    for first in (0, ROWS - HALO):
        sides = []
        for side, edge_ref in enumerate((west_ref, east_ref)):
            begin = HALO * (REST + side * HALO)
            rolled = pltpu.roll(edge_ref[...].astype(F32), (begin - first * HALO) % 128, 1)
            inside = jnp.logical_and(lane >= begin, lane < begin + HALO * HALO)
            sides.append(jnp.where(inside, rolled, 0.0))
        beyond.append(sides[0] + sides[1])
    for ref, north in ((pay0_ref, 1 - odd), (pay1_ref, odd)):
        rest = []
        for k in range(HALO):
            row = rows_ref[(ROWS - HALO) * north + k]
            ref[k * CH : (k + 1) * CH, :] = row[:, :MAIN]
            rest.append(row[:, MAIN:COLS].astype(F32))
        tail = jnp.concatenate(rest + [jnp.zeros((CH, 128 - HALO * REST), F32)], axis=1)
        ref[HALO * CH :, :] = tail_out(tail + jnp.where(north == 1, beyond[1], beyond[0]))


def weight_kernel(w_in, w_down, w_mid, w_up, w_out, in_ref, down_ref, mid_ref, up_ref, out_ref):
    for ref in (in_ref, down_ref, mid_ref, up_ref, out_ref):
        ref[...] = jnp.zeros(ref.shape, BF16)
    for raw, ref in ((w_in, in_ref), (w_down, down_ref), (w_mid, mid_ref), (w_up, up_ref)):
        for t in range(raw.shape[0]):
            ref[t, : raw.shape[1], :HIDDEN] = raw[t]
    for a in range(3):
        for b in range(3):
            for r in range(3):
                t = 3 * (a + r) + b
                out_ref[r * CH : r * CH + CHANNELS, t * HID : t * HID + HIDDEN] = w_out[3 * a + b]


def flip(block):
    n = block.shape[1]
    return jnp.concatenate([block, jnp.zeros((128 - CH, n), F32)], axis=0).T


def pack(t_ref, a_ref, ai):
    lane = lax.broadcasted_iota(jnp.int32, (PIX, 128), 1)
    odd_left, even, odd, even_right = (t_ref[pl.ds(3 + s, PIX, stride=2), :] for s in range(4))
    even80, odd80 = pltpu.roll(even, CH, 1), pltpu.roll(odd, CH, 1)
    for p, (left, mid, right) in enumerate(((odd_left, even80, odd), (even, odd80, even_right))):
        low = jnp.where(lane < CH, left, mid)
        high = jnp.where(lane < 2 * CH - 128, mid, pltpu.roll(right, 2 * CH - 128, 1))
        a_ref[ai, p * PIX : (p + 1) * PIX, :] = jnp.concatenate([low, high], axis=1).astype(BF16)


def straight(t, n):
    return t


def first_rows(a_ref, f_ref, w_ref, fr, n, tap):
    w = []
    for a in range(3):
        w += [w_ref[tap(3 * a + b, 9)] for b in range(3)] + [jnp.zeros((HID - 3 * CH, HID), BF16)]
    w = jnp.concatenate(w, axis=0)
    for q in range(n):
        taps = jnp.concatenate([a_ref[fr + q + a] for a in range(3)], axis=1)
        f_ref[fr + q] = gelu(jnp.dot(taps, w, preferred_element_type=F32)).astype(BF16)


def coarse_rows(f_ref, c_ref, w_ref, ci, n, tap, held):
    w = jnp.concatenate([w_ref[tap(t, 4)] for t in range(4)], axis=1)
    pieces = []
    for q in range(n):
        piece = [f_ref[2 * (ci + q) + a, b * PIX : (b + 1) * PIX, :] for a in range(2) for b in range(2)]
        pieces.append(jnp.concatenate(piece, axis=1))
    coarse = gelu(dot_nt(jnp.concatenate(pieces, axis=0), w))
    if held is not None:
        coarse = coarse * held
    for q in range(n):
        one = coarse[q * PIX : (q + 1) * PIX]
        planes = [pltpu.roll(one, 1, 0), one, pltpu.roll(one, PIX - 1, 0)]
        c_ref[ci + q] = jnp.concatenate(planes, axis=1).astype(BF16)


def mid_rows(c_ref, f_ref, j_ref, mid_ref, up_ref, mi, n, tap, held):
    taps = [c_ref[pl.ds(mi + a, n)].reshape(n * PIX, 3 * HID) for a in range(3)]
    w = jnp.concatenate([mid_ref[tap(t, 9)] for t in range(9)], axis=1)
    middle = gelu(dot_nt(jnp.concatenate(taps, axis=1), w)).astype(BF16)
    for a in range(2):
        grown = [dot_nt(middle, up_ref[tap(2 * a + b, 4)]) for b in range(2)]
        for q in range(n):
            row = 2 * (mi + q) + a
            halves = []
            for b in range(2):
                first = f_ref[row + 2, b * PIX : (b + 1) * PIX, :].astype(F32)
                half = gelu(grown[b][q * PIX : (q + 1) * PIX]) + first
                halves.append(half * held if held is not None and q == 0 else half)
            even, odd = halves
            planes = (pltpu.roll(odd, 1, 0), even, odd, pltpu.roll(even, PIX - 1, 0))
            for s, plane in enumerate(planes):
                j_ref[row, s * PIX : (s + 1) * PIX, :] = plane.astype(BF16)


A_KEPT = (5, 6, 15, 16)
F_KEPT = (5, 6, 7, 12, 13, 14)
C_KEPT = (3, 4, 5, 6)
J_KEPT = (6, 7, 8, 9)
KEPT = (A_KEPT, F_KEPT, C_KEPT, J_KEPT)
BLOCKS = ((2 * PIX, HID), (2 * PIX, HID), (PIX, 3 * HID), (4 * PIX, HID))
HELD = [pltpu.VMEM((n,) + block, BF16) for n, block in zip((22, 20, 10, 16), BLOCKS)]


def inner_kernel(rows_ref, west_ref, east_ref, in_ref, down_ref, mid_ref, up_ref, *refs):
    outs, (t_refs, edge_ref, a_ref, f_ref, c_ref, j_ref) = refs[:4], refs[4:]
    edge_ref[0] = flip(west_ref[...].astype(F32))
    edge_ref[1] = flip(east_ref[...].astype(F32))

    def own_rows(i, carry):
        for q in range(2):
            t_ref, r = t_refs.at[q], 2 * i + q
            t_ref[8 : 8 + LANES, :] = flip(rows_ref[r].astype(F32))
            t_ref[8 - HALO : 8, :] = edge_ref[0, pl.ds(r * HALO, HALO), :]
            t_ref[8 + COLS : 8 + COLS + HALO, :] = edge_ref[1, pl.ds(r * HALO, HALO), :]
            pack(t_ref, a_ref, r + HALO)
        return carry

    lax.fori_loop(0, ROWS // 2, own_rows, 0)

    def first_group(i, carry):
        first_rows(a_ref, f_ref, in_ref, 5 + 2 * i, 2, straight)
        return carry

    lax.fori_loop(0, 5, first_group, 0)
    coarse_rows(f_ref, c_ref, down_ref, 3, 4, straight, None)
    mid_rows(c_ref, f_ref, j_ref, mid_ref, up_ref, 3, 2, straight, None)
    for ref, out_ref, kept in zip((a_ref, f_ref, c_ref, j_ref), outs, KEPT):
        for i, row in enumerate(kept):
            out_ref[i] = ref[row]


def outer_kernel(
    seam_ref, got0_ref, got1_ref, fold2_ref, fold3_ref, own_ref, in_ref, down_ref, mid_ref, up_ref, w_out_ref,
    state_ref, mask_ref, a_in, f_in, c_in, j_in, out_ref, t_refs, edge_ref, a_ref, f_ref, c_ref, j_ref, u_ref,
):
    n_lat, n_lon = lax.axis_size("lat"), lax.axis_size("lon")
    lat, lon = lax.axis_index("lat"), lax.axis_index("lon")
    bottom, top = lat == 0, lat == n_lat - 1
    keep = jnp.where(bottom, 0.0, 1.0).astype(F32)
    for ref, in_ref_, kept in zip((a_ref, f_ref, c_ref, j_ref), (a_in, f_in, c_in, j_in), KEPT):
        for i, row in enumerate(kept):
            ref[row] = in_ref_[i]
    edge_ref[0] = flip(tail_in(got0_ref))
    edge_ref[1] = flip(tail_in(got1_ref))

    def halo_row(t_ref, ref, side, k, ai):
        t_ref[8 : 8 + MAIN, :] = flip(ref[pl.ds(pl.multiple_of(k * CH, CH), CH), :].astype(F32))
        t_ref[8 + MAIN : 8 + COLS, :] = edge_ref[side, pl.ds(k * REST, REST), :]
        t_ref[8 - HALO : 8, :] = edge_ref[side, pl.ds(HALO * REST + k * HALO, HALO), :]
        t_ref[8 + COLS : 8 + COLS + HALO, :] = edge_ref[side, pl.ds(HALO * (REST + HALO) + k * HALO, HALO), :]
        pack(t_ref, a_ref, ai)

    odd = lax.rem(lat, 2)
    at = (1 - odd) * (ROWS + HALO), odd * (ROWS + HALO)
    t_refs[...] = jnp.zeros(t_refs.shape, F32)

    def halo_rows(k, carry):
        halo_row(t_refs.at[0], got0_ref, 0, k, at[0] + k)
        halo_row(t_refs.at[1], got1_ref, 1, k, at[1] + k)
        return carry

    lax.fori_loop(0, HALO, halo_rows, 0)

    @pl.when(bottom)
    def _():
        a_ref[0:HALO] = jnp.zeros((HALO, 2 * PIX, HID), BF16)

    @pl.when(top)
    def _():
        circle = n_lon * COLS
        span = 288
        column = lax.broadcasted_iota(jnp.int32, (span, 128), 0) - 8 + COLS * lon
        source = lax.rem(seam_ref[0] - column + 3 * circle, circle)
        spot = lax.broadcasted_iota(jnp.int32, (span, 128), 1)

        def fold_row(k, carry):
            kk = HALO - 1 - k
            total = jnp.zeros((span, CH), F32)
            for d, ref in enumerate((own_ref, got1_ref, fold2_ref, fold3_ref)):
                place = source - lax.bitwise_xor(lon, d) * COLS
                hot = [(place == spot), (place == spot + 128)]
                inside = jnp.logical_and(place >= MAIN, place < COLS)
                hot.append(jnp.logical_and(inside, place - MAIN + kk * REST == spot))
                hot = jnp.concatenate([jnp.where(h, 1.0, 0.0).astype(BF16) for h in hot], axis=1)
                main = ref[pl.ds(pl.multiple_of(kk * CH, CH), CH), :]
                total += dot_nt(hot, jnp.concatenate([main, tail_in(ref).astype(BF16)], axis=1))
            t_refs[0, 0:span, :] = jnp.concatenate([total, jnp.zeros((span, 128 - CH), F32)], axis=1)
            pack(t_refs.at[0], a_ref, ROWS + HALO + k)
            return carry

        lax.fori_loop(0, HALO, fold_row, 0)

    def first_group(i, carry):
        turned = jnp.logical_and(top, i == 1)
        tap = lambda t, n: jnp.where(turned, n - 1 - t, t)
        first_rows(a_ref, f_ref, in_ref, 4 + 11 * i, 1, straight)
        first_rows(a_ref, f_ref, in_ref, 16 * i, 4, tap)
        coarse_rows(f_ref, c_ref, down_ref, 8 * i, 2, tap, jnp.where(i == 0, keep, 1.0))
        coarse_rows(f_ref, c_ref, down_ref, 2 + 5 * i, 1, straight, None)
        return carry

    lax.fori_loop(0, 2, first_group, 0)

    def mid_group(i, carry):
        held = jnp.where(i == 0, keep, 1.0)
        mid_rows(c_ref, f_ref, j_ref, mid_ref, up_ref, 5 * i, 3, straight, held)
        return carry

    lax.fori_loop(0, 2, mid_group, 0)

    @pl.when(top)
    def _():
        mid_rows(c_ref, f_ref, j_ref, mid_ref, up_ref, 7, 1, lambda t, n: n - 1 - t, None)

    def out_rows(g, carry):
        groups = []
        for q in range(2):
            jr = 6 * g + 3 * q + 1
            taps = [j_ref[jr + i, b * PIX : (b + 2) * PIX, :] for i in range(5) for b in range(3)]
            groups.append(jnp.concatenate(taps, axis=1))
        deltas = dot_nt(jnp.concatenate(groups, axis=0), w_out_ref[...])
        for q in range(2):
            flipped = []
            for t in range(2):
                for p in range(2):
                    begin = (2 * q + p) * PIX
                    half = deltas[begin : begin + PIX, t * 128 : (t + 1) * 128]
                    u_ref[pl.ds((2 * q + t) * TROWS + 4 + p, PIX, stride=2), :] = half
                begin = (2 * q + t) * TROWS + 8
                flipped.append(u_ref[begin : begin + LANES, :].T)
            flipped = jnp.concatenate(flipped, axis=0)
            for i in range(3):
                r = 6 * g + 3 * q + i
                delta = flipped[i * CH : i * CH + CHANNELS, :COLS]
                cover = jnp.concatenate([mask_ref[r].astype(F32)] * VARS, axis=0)
                out_ref[r] = ((state_ref[r].astype(F32) + delta) * cover).astype(BF16)
        return carry

    lax.fori_loop(0, 2, out_rows, 0)


def body(state, sea_mask, seam, w_in, w_down, w_mid, w_up, w_out):
    n_lat, n_lon = lax.axis_size("lat"), lax.axis_size("lon")
    ring = lambda n, d: [(i, (i + d) % n) for i in range(n)]
    state, sea_mask = jnp.swapaxes(state, 0, 1), jnp.swapaxes(sea_mask, 0, 1)
    flat = lambda w: w.reshape((-1,) + w.shape[2:])
    edge = (CH, 128)
    rows, east_going, west_going, fold = call(
        edge_kernel, [HBM] * 2, (state, sea_mask), [(ROWS, CH, LANES), edge, edge, PAYLOAD],
        [
            pltpu.VMEM((ROWS, CHANNELS, COLS), BF16),
            pltpu.VMEM((ROWS, LEVELS, COLS), jnp.int32),
            pltpu.SemaphoreType.DMA((2, ROWS // CHUNK)),
        ],
        1.5, 12,
    )
    west = lax.ppermute(east_going, "lon", ring(n_lon, 1))
    east = lax.ppermute(west_going, "lon", ring(n_lon, -1))

    def swap(begin, d):
        pairs = []
        for i in range(n_lat):
            for j in range(n_lon):
                mate = i + 1 if (i - begin) % 2 == 0 else i - 1
                if begin < n_lat and 0 <= mate < n_lat:
                    pairs.append((i * n_lon + j, mate * n_lon + j))
                else:
                    pairs.append((i * n_lon + j, i * n_lon + (j ^ (d if i == n_lat - 1 else 1))))
        return pairs

    axes = ("lat", "lon")
    folds = [lax.ppermute(fold, axes, swap(n_lat, d)) for d in (2, 3)]
    laid = call(
        weight_kernel, [VMEM] * 5, (flat(jnp.swapaxes(w_in, 2, 3)), flat(w_down), flat(w_mid), flat(w_up), flat(w_out)),
        [(9, CH, HID), (4, HID, HID), (9, HID, HID), (4, HID, HID), (HID, 15 * HID)], [], 1.5, 16,
    )
    pay0, pay1 = call(payload_kernel, [VMEM] * 3, (rows, west, east), [PAYLOAD] * 2, [], 0.5, 8)
    got0 = lax.ppermute(pay0, axes, swap(0, 1))
    got1 = lax.ppermute(pay1, axes, swap(1, 1))
    kept = [(len(k),) + block for k, block in zip(KEPT, BLOCKS)]
    inner = call(
        inner_kernel, [VMEM] * 7, (rows, west, east, *laid[:4]), kept,
        [pltpu.VMEM((2, TROWS, 128), F32), pltpu.VMEM((2, 128, 128), F32)] + HELD, 6, 30,
    )
    (out,) = call(
        outer_kernel, [SMEM] + [VMEM] * 16,
        (seam, got0, got1, *folds, fold, *laid, state, sea_mask, *inner), [(ROWS, CHANNELS, COLS)],
        [pltpu.VMEM((2, TROWS, 128), F32), pltpu.VMEM((2, 128, 128), F32)] + HELD + [pltpu.VMEM((4 * TROWS, 128), F32)],
        12, 36,
    )
    return jnp.swapaxes(out, 0, 1)


def solution(mesh):
    return jax.shard_map(
        body,
        mesh=mesh,
        in_specs=(P(None, "lat", "lon"), P(None, "lat", "lon"), P(), P(), P(), P(), P(), P()),
        out_specs=P(None, "lat", "lon"),
        check_vma=False,
    )
```

```python
import functools

import jax
import jax.numpy as jnp
from jax import lax
from jax.experimental import pallas as pl
from jax.experimental.pallas import tpu as pltpu
from jax.sharding import PartitionSpec as P

VARS, LEVELS, CHANNELS, HIDDEN = 4, 19, 76, 200
ROWS, COLS = 12, 270
HALO = 5
CH = 80
LANES = 384
MAIN = 256
REST = COLS - MAIN
PAYLOAD = (HALO * CH + CH // 2, MAIN)
PIX = 144
HID = 256
TROWS = 408
FOLD_REST = COLS + 2 * HALO - MAIN
CHUNK = 3
F32, BF16 = jnp.float32, jnp.bfloat16
VMEM = pl.BlockSpec(memory_space=pltpu.VMEM)
HBM = pl.BlockSpec(memory_space=pltpu.HBM)
SMEM = pl.BlockSpec(memory_space=pltpu.SMEM)


def dot_nt(a, b):
    return lax.dot_general(a, b, (((1,), (1,)), ((), ())), preferred_element_type=F32)


def gelu(x):
    inner = x * (0.7978845608028654 + 0.035677408136300125 * (x * x))
    half = 0.5 * x
    return half + half * jnp.tanh(inner)


def cost(us):
    return pl.CostEstimate(flops=int(us * 1e9), bytes_accessed=int(us * 3e6), transcendentals=0)


def call(kernel, ins, operands, outs, scratch, us, mib):
    return pl.pallas_call(
        kernel,
        out_shape=tuple(jax.ShapeDtypeStruct(shape, BF16) for shape in outs),
        in_specs=ins,
        out_specs=(VMEM,) * len(outs),
        scratch_shapes=scratch,
        cost_estimate=cost(us),
        compiler_params=pltpu.CompilerParams(vmem_limit_bytes=mib * 2**20),
    )(*operands)


def masked_row(state_ref, mask_ref, r):
    cover = mask_ref[r].astype(F32)
    row = state_ref[r].astype(F32) * jnp.concatenate([cover] * VARS, axis=0)
    row = jnp.concatenate([row, jnp.zeros((CHANNELS, LANES - COLS), F32)], axis=1)
    return jnp.concatenate([row, jnp.zeros((CH - CHANNELS, LANES), F32)], axis=0)


def tail_out(tail):
    return jnp.concatenate([tail[: CH // 2], tail[CH // 2 :]], axis=1).astype(BF16)


def tail_in(payload_ref):
    low = payload_ref[HALO * CH :, :]
    return jnp.concatenate([low[:, :128], low[:, 128:]], axis=0).astype(F32)


def edge_kernel(state_hbm, mask_hbm, east_ref, west_ref, high_ref, state_ref, mask_ref, sems):
    copies = []
    for i in range(ROWS // CHUNK):
        rows = pl.ds(i * CHUNK, CHUNK)
        for j, (hbm, ref) in enumerate(((mask_hbm, mask_ref), (state_hbm, state_ref))):
            copies.append(pltpu.make_async_copy(hbm.at[rows], ref.at[rows], sems.at[j, i]))
            copies[-1].start()
    low, high = [], []
    for r in range(ROWS):
        if r % CHUNK == 0:
            for copy in copies[2 * (r // CHUNK) : 2 * (r // CHUNK) + 2]:
                copy.wait()
        for held, columns in ((low, slice(0, HALO)), (high, slice(COLS - HALO, COLS))):
            cover = mask_ref[r, :, columns].astype(F32)
            masked = state_ref[r, :, columns].astype(F32) * jnp.concatenate([cover] * VARS, axis=0)
            held.append(jnp.concatenate([masked, jnp.zeros((CH - CHANNELS, HALO), F32)], axis=0))
        k = r - (ROWS - HALO)
        if k >= 0:
            high_ref[k * CH : (k + 1) * CH, :] = masked_row(state_ref, mask_ref, r).astype(BF16)
    rest = [jnp.zeros((CH, 128 - ROWS * HALO), F32)]
    west_ref[...] = jnp.concatenate(low + rest, axis=1).astype(BF16)
    east_ref[...] = jnp.concatenate(high + rest, axis=1).astype(BF16)


def fill_payload(rows_ref, west_ref, east_ref, ref, north):
    lane = lax.broadcasted_iota(jnp.int32, (CH, 128), 1)
    sides = []
    for side, edge_ref in enumerate((west_ref, east_ref)):
        begin = HALO * (REST + side * HALO)
        edge = edge_ref[...].astype(F32)
        rolled = [pltpu.roll(edge, (begin - first * HALO) % 128, 1) for first in (0, ROWS - HALO)]
        inside = jnp.logical_and(lane >= begin, lane < begin + HALO * HALO)
        sides.append(jnp.where(inside, jnp.where(north == 1, rolled[1], rolled[0]), 0.0))
    rest = []
    for k in range(HALO):
        row = rows_ref[(ROWS - HALO) * north + k]
        ref[k * CH : (k + 1) * CH, :] = row[:, :MAIN]
        rest.append(row[:, MAIN:COLS].astype(F32))
    tail = jnp.concatenate(rest + [jnp.zeros((CH, 128 - HALO * REST), F32)], axis=1)
    ref[HALO * CH :, :] = tail_out(tail + sides[0] + sides[1])


def payload_kernel(seam_ref, rows_ref, west_ref, east_ref, high_ref, mate_ref, pay_ref, kept_ref):
    lat, lon = lax.axis_index("lat"), lax.axis_index("lon")
    top = lat == lax.axis_size("lat") - 1

    @pl.when(top)
    def _():
        fill_fold(seam_ref, high_ref, mate_ref, lax.bitwise_xor(lon, 2), pay_ref)
        fill_fold(seam_ref, high_ref, mate_ref, lon, kept_ref)

    @pl.when(jnp.logical_not(top))
    def _():
        fill_payload(rows_ref, west_ref, east_ref, pay_ref, lax.rem(lat, 2))


def pack_kernel(rows_ref, west_ref, east_ref, in_ref, packed_ref, pay_ref, f_ref, t_refs, edge_ref):
    fill_payload(rows_ref, west_ref, east_ref, pay_ref, 1 - lax.rem(lax.axis_index("lat"), 2))
    edge_ref[0] = flip(west_ref[...].astype(F32))
    edge_ref[1] = flip(east_ref[...].astype(F32))

    for r in range(ROWS):
        t_ref, edge = t_refs.at[r % 2], slice(r * HALO, (r + 1) * HALO)
        t_ref[8 : 8 + LANES, :] = flip(rows_ref[r].astype(F32))
        t_ref[8 - HALO : 8, :] = edge_ref[0, edge, :]
        t_ref[8 + COLS : 8 + COLS + HALO, :] = edge_ref[1, edge, :]
        pack(t_ref, packed_ref, r)
    first_rows(packed_ref, HALO, f_ref, F_FIRST, in_ref, F_FIRST, F_ROWS, straight)


def fill_fold(seam_ref, high_ref, mate_ref, target, ref):
    n_lon = lax.axis_size("lon")
    lon = lax.axis_index("lon")
    circle = n_lon * COLS
    held = jnp.concatenate([high_ref[...], mate_ref[...]], axis=1)
    spot = lax.broadcasted_iota(jnp.int32, (2 * LANES, LANES), 0)
    place = spot + jnp.where(spot < LANES, lon * COLS, lax.bitwise_xor(lon, 1) * COLS - LANES)
    column = lax.broadcasted_iota(jnp.int32, (2 * LANES, LANES), 1) - HALO + target * COLS
    source = lax.rem(seam_ref[0] - column + 3 * circle, circle)
    hot = jnp.where(place == source, 1.0, 0.0).astype(BF16)
    rows = jnp.dot(held, hot, preferred_element_type=F32)
    ref[: HALO * CH, :] = rows[:, :MAIN].astype(BF16)
    lane = lax.broadcasted_iota(jnp.int32, (CH, 128), 1)
    tail = jnp.zeros((CH, 128), F32)
    for k in range(HALO):
        shift = FOLD_REST * k
        rolled = pltpu.roll(rows[k * CH : (k + 1) * CH, MAIN:], shift, 1)
        tail += jnp.where(jnp.logical_and(lane >= shift, lane < shift + FOLD_REST), rolled, 0.0)
    ref[HALO * CH :, :] = tail_out(tail)


def ready_kernel(after_ref, state_ref, mask_ref, w_in, w_down, w_mid, w_up, w_out, rows_ref, *padded):
    for r in range(ROWS):
        rows_ref[r] = masked_row(state_ref, mask_ref, r).astype(BF16)
    weight_kernel(w_in, w_down, w_mid, w_up, w_out, *padded)


def weight_kernel(w_in, w_down, w_mid, w_up, w_out, in_ref, down_ref, mid_ref, up_ref, out_ref):
    for ref in (in_ref, down_ref, mid_ref, up_ref, out_ref):
        ref[...] = jnp.zeros(ref.shape, BF16)
    for raw, ref in ((w_in, in_ref), (w_down, down_ref), (w_mid, mid_ref), (w_up, up_ref)):
        for t in range(raw.shape[0]):
            ref[t, : raw.shape[1], :HIDDEN] = raw[t]
    for a in range(3):
        for b in range(3):
            for r in range(3):
                t = 3 * (a + r) + b
                out_ref[r * CH : r * CH + CHANNELS, t * HID : t * HID + HIDDEN] = w_out[3 * a + b]


def flip(block):
    n = block.shape[1]
    return jnp.concatenate([block, jnp.zeros((128 - CH, n), F32)], axis=0).T


def pack(t_ref, a_ref, ai):
    lane = lax.broadcasted_iota(jnp.int32, (PIX, 128), 1)
    odd_left, even, odd, even_right = (t_ref[pl.ds(3 + s, PIX, stride=2), :] for s in range(4))
    even80, odd80 = pltpu.roll(even, CH, 1), pltpu.roll(odd, CH, 1)
    for p, (left, mid, right) in enumerate(((odd_left, even80, odd), (even, odd80, even_right))):
        low = jnp.where(lane < CH, left, mid)
        high = jnp.where(lane < 2 * CH - 128, mid, pltpu.roll(right, 2 * CH - 128, 1))
        a_ref[ai, p * PIX : (p + 1) * PIX, :] = jnp.concatenate([low, high], axis=1).astype(BF16)


def straight(t, n):
    return t


def first_rows(a_ref, begin, f_ref, f_begin, w_ref, fr, n, tap):
    w = []
    for a in range(3):
        w += [w_ref[tap(3 * a + b, 9)] for b in range(3)] + [jnp.zeros((HID - 3 * CH, HID), BF16)]
    w = jnp.concatenate(w, axis=0)
    for q in range(n):
        taps = jnp.concatenate([a_ref[fr + q + a - begin] for a in range(3)], axis=1)
        f_ref[fr + q - f_begin] = gelu(jnp.dot(taps, w, preferred_element_type=F32)).astype(BF16)


def coarse_rows(f_ref, f_begin, c_ref, w_ref, ci, n, tap, held):
    w = jnp.concatenate([w_ref[tap(t, 4)] for t in range(4)], axis=1)
    pieces = []
    for q in range(n):
        piece = [f_ref[2 * (ci + q) + a - f_begin, b * PIX : (b + 1) * PIX, :] for a in range(2) for b in range(2)]
        pieces.append(jnp.concatenate(piece, axis=1))
    coarse = gelu(dot_nt(jnp.concatenate(pieces, axis=0), w))
    if held is not None:
        coarse = coarse * held
    for q in range(n):
        one = coarse[q * PIX : (q + 1) * PIX]
        planes = [pltpu.roll(one, 1, 0), one, pltpu.roll(one, PIX - 1, 0)]
        c_ref[ci + q] = jnp.concatenate(planes, axis=1).astype(BF16)


def mid_rows(c_ref, f_ref, f_begin, j_ref, mid_ref, up_ref, mi, n, tap, held):
    taps = [c_ref[pl.ds(mi + a, n)].reshape(n * PIX, 3 * HID) for a in range(3)]
    w = jnp.concatenate([mid_ref[tap(t, 9)] for t in range(9)], axis=1)
    middle = gelu(dot_nt(jnp.concatenate(taps, axis=1), w)).astype(BF16)
    for a in range(2):
        grown = [dot_nt(middle, up_ref[tap(2 * a + b, 4)]) for b in range(2)]
        for q in range(n):
            row = 2 * (mi + q) + a
            halves = []
            for b in range(2):
                first = f_ref[row + 2 - f_begin, b * PIX : (b + 1) * PIX, :].astype(F32)
                half = gelu(grown[b][q * PIX : (q + 1) * PIX]) + first
                halves.append(half * held if held is not None and q == 0 else half)
            even, odd = halves
            planes = (pltpu.roll(odd, 1, 0), even, odd, pltpu.roll(even, PIX - 1, 0))
            for s, plane in enumerate(planes):
                j_ref[row, s * PIX : (s + 1) * PIX, :] = plane.astype(BF16)


F_FIRST, F_ROWS = 5, 10
C_KEPT = (3, 4, 5, 6)
J_KEPT = (6, 7, 8, 9)
KEPT = (C_KEPT, J_KEPT)
PACKED = (2 * PIX, HID)
BLOCKS = ((PIX, 3 * HID), (4 * PIX, HID))
HELD = [pltpu.VMEM((n,) + block, BF16) for n, block in zip((10, 16), BLOCKS)]


def inner_kernel(f_ref, down_ref, mid_ref, up_ref, *refs):
    outs, (c_ref, j_ref) = refs[:2], refs[2:]
    coarse_rows(f_ref, F_FIRST, c_ref, down_ref, 3, 4, straight, None)
    mid_rows(c_ref, f_ref, F_FIRST, j_ref, mid_ref, up_ref, 3, 2, straight, None)
    for ref, out_ref, kept in zip((c_ref, j_ref), outs, KEPT):
        for i, row in enumerate(kept):
            out_ref[i] = ref[row]


def outer_kernel(second, *refs):
    got_ref, refs = refs[0], refs[1:]
    if second:
        half_ref, refs = refs[0], refs[1:]
    else:
        kept_ref, refs = refs[0], refs[1:]
    in_ref, down_ref, mid_ref, up_ref, w_out_ref, state_ref, mask_ref, packed_ref, f_in, c_in, j_in, out_ref = refs[:12]
    t_refs, edge_ref, a_ref, f_ref, c_ref, j_ref, u_ref = refs[12:]
    lat = lax.axis_index("lat")
    bottom, top = lat == 0, lat == lax.axis_size("lat") - 1

    def side(north):
        for q in range(2):
            a_ref[5 + 10 * north + q] = packed_ref[10 * north + q]
            c_ref[3 + 2 * north + q] = c_in[2 * north + q]
        for q in range(3):
            f_ref[5 + 7 * north + q] = f_in[7 * north + q]
            j_ref[6 + north + q] = j_in[north + q]
        edge_ref[0] = flip(tail_in(got_ref))
        t_refs[...] = jnp.zeros(t_refs.shape, F32)
        for k in range(HALO):
            t_ref = t_refs.at[k % 2]
            t_ref[8 : 8 + MAIN, :] = flip(got_ref[k * CH : (k + 1) * CH, :].astype(F32))
            for begin, at, n in ((0, MAIN, REST), (HALO * REST, -HALO, HALO), (HALO * (REST + HALO), COLS, HALO)):
                t_ref[8 + at : 8 + at + n, :] = edge_ref[0, begin + k * n : begin + (k + 1) * n, :]
            pack(t_ref, a_ref, (ROWS + HALO) * north + k)

        if not second and not north:

            @pl.when(bottom)
            def _():
                a_ref[0:HALO] = jnp.zeros((HALO,) + PACKED, BF16)

        if not second and north:
            @pl.when(top)
            def _():
                edge_ref[0] = flip(tail_in(got_ref) + tail_in(kept_ref))
                for k in range(HALO):
                    kk = HALO - 1 - k
                    rows = slice(kk * CH, (kk + 1) * CH)
                    t_ref = t_refs.at[k % 2]
                    t_ref[8 - HALO : 8 - HALO + MAIN, :] = flip(got_ref[rows, :].astype(F32) + kept_ref[rows, :].astype(F32))
                    rest = edge_ref[0, FOLD_REST * kk : FOLD_REST * (kk + 1), :]
                    t_ref[8 - HALO + MAIN : 8 + COLS + HALO, :] = rest
                    pack(t_ref, a_ref, ROWS + HALO + k)

        keep, turn = None, straight
        if not second and north:
            turn = lambda t, n: jnp.where(top, n - 1 - t, t)
        elif not second:
            keep = jnp.where(bottom, 0.0, 1.0).astype(F32)
        first_rows(a_ref, 0, f_ref, 0, in_ref, 4 + 11 * north, 1, straight)
        first_rows(a_ref, 0, f_ref, 0, in_ref, 16 * north, 4, turn)
        coarse_rows(f_ref, 0, c_ref, down_ref, 8 * north, 2, turn, keep)
        coarse_rows(f_ref, 0, c_ref, down_ref, 2 + 5 * north, 1, straight, None)
        mid_rows(c_ref, f_ref, 0, j_ref, mid_ref, up_ref, 5 * north, 3, straight, keep)

        if not second and north:

            @pl.when(top)
            def _():
                mid_rows(c_ref, f_ref, 0, j_ref, mid_ref, up_ref, 7, 1, lambda t, n: n - 1 - t, None)

        groups = []
        for q in range(2):
            taps = [j_ref[6 * north + 3 * q + 1 + i, b * PIX : (b + 2) * PIX, :] for i in range(5) for b in range(3)]
            groups.append(jnp.concatenate(taps, axis=1))
        deltas = dot_nt(jnp.concatenate(groups, axis=0), w_out_ref[...])
        for q in range(2):
            flipped = []
            for t in range(2):
                for p in range(2):
                    begin = (2 * q + p) * PIX
                    half = deltas[begin : begin + PIX, t * 128 : (t + 1) * 128]
                    u_ref[pl.ds((2 * q + t) * TROWS + 4 + p, PIX, stride=2), :] = half
                begin = (2 * q + t) * TROWS + 8
                flipped.append(u_ref[begin : begin + LANES, :].T)
            flipped = jnp.concatenate(flipped, axis=0)
            for i in range(3):
                r = 6 * north + 3 * q + i
                delta = flipped[i * CH : i * CH + CHANNELS, :COLS]
                cover = jnp.concatenate([mask_ref[r].astype(F32)] * VARS, axis=0)
                out = ((state_ref[r].astype(F32) + delta) * cover).astype(BF16)
                out_ref[r if second else 3 * q + i] = out
        if second:
            for q in range(6):
                out_ref[6 * (1 - north) + q] = half_ref[q]

    for north in range(2):
        pl.when(lax.rem(lat, 2) == (1 - north if second else north))(functools.partial(side, north))


def body(state, sea_mask, seam, w_in, w_down, w_mid, w_up, w_out):
    n_lat, n_lon = lax.axis_size("lat"), lax.axis_size("lon")
    ring = lambda n, d: [(i, (i + d) % n) for i in range(n)]
    state, sea_mask = jnp.swapaxes(state, 0, 1), jnp.swapaxes(sea_mask, 0, 1)
    flat = lambda w: w.reshape((-1,) + w.shape[2:])
    edge = (CH, 128)
    east_going, west_going, high = call(
        edge_kernel, [HBM] * 2, (state, sea_mask), [edge, edge, (HALO * CH, LANES)],
        [
            pltpu.VMEM((ROWS, CHANNELS, COLS), BF16),
            pltpu.VMEM((ROWS, LEVELS, COLS), jnp.int32),
            pltpu.SemaphoreType.DMA((2, ROWS // CHUNK)),
        ],
        1, 60,
    )
    west = lax.ppermute(east_going, "lon", ring(n_lon, 1))
    east = lax.ppermute(west_going, "lon", ring(n_lon, -1))

    axes = ("lat", "lon")
    within = [(i, i ^ 1) for i in range(n_lat * n_lon)]

    def swap(begin):
        pairs = []
        for i in range(n_lat):
            for j in range(n_lon):
                mate = i + 1 if (i - begin) % 2 == 0 else i - 1
                target = mate * n_lon + j if 0 <= mate < n_lat else i * n_lon + (j ^ 2)
                pairs.append((i * n_lon + j, target))
        return pairs

    mate = lax.ppermute(high, axes, within)
    rows, *laid = call(
        ready_kernel, [VMEM] * 8,
        (west_going, state, sea_mask, flat(jnp.swapaxes(w_in, 2, 3)), flat(w_down), flat(w_mid), flat(w_up), flat(w_out)),
        [
            (ROWS, CH, LANES),
            (9, CH, HID), (4, HID, HID), (9, HID, HID), (4, HID, HID), (HID, 15 * HID),
        ],
        [], 1.5, 16,
    )
    pay, kept = call(
        payload_kernel, [SMEM] + [VMEM] * 5, (seam, rows, west, east, high, mate), [PAYLOAD] * 2, [], 0.4, 8,
    )
    got = lax.ppermute(pay, axes, swap(1))
    turning = [pltpu.VMEM((2, TROWS, 128), F32), pltpu.VMEM((2, 128, 128), F32)]
    packed, pay, f_own = call(
        pack_kernel, [VMEM] * 4, (rows, west, east, laid[0]),
        [(ROWS,) + PACKED, PAYLOAD, (F_ROWS,) + PACKED], turning, 3.5, 18,
    )
    got_later = lax.ppermute(pay, axes, swap(0))
    handed = [(len(k),) + block for k, block in zip(KEPT, BLOCKS)]
    inner = call(inner_kernel, [VMEM] * 4, (f_own, *laid[1:4]), handed, HELD, 1.7, 24)
    scratch = turning + [pltpu.VMEM((n,) + PACKED, BF16) for n in (22, 20)] + HELD + [pltpu.VMEM((4 * TROWS, 128), F32)]
    shared = (*laid, state, sea_mask, packed, f_own, *inner)
    (half,) = call(
        functools.partial(outer_kernel, False), [VMEM] * 13, (got, kept, *shared), [(ROWS // 2, CHANNELS, COLS)],
        scratch, 5, 30,
    )
    (out,) = call(
        functools.partial(outer_kernel, True), [VMEM] * 13, (got_later, half, *shared), [(ROWS, CHANNELS, COLS)],
        scratch, 6, 30,
    )
    return jnp.swapaxes(out, 0, 1)


def solution(mesh):
    return jax.shard_map(
        body,
        mesh=mesh,
        in_specs=(P(None, "lat", "lon"), P(None, "lat", "lon"), P(), P(), P(), P(), P(), P()),
        out_specs=P(None, "lat", "lon"),
        check_vma=False,
    )
```

```python
import functools

import jax
import jax.numpy as jnp
from jax import lax
from jax.experimental import pallas as pl
from jax.experimental.pallas import tpu as pltpu
from jax.sharding import PartitionSpec as P

VARS, LEVELS, CHANNELS, HIDDEN = 4, 19, 76, 200
ROWS, COLS = 12, 270
HALO = 5
CH = 80
LANES = 384
MAIN = 256
REST = COLS - MAIN
PAYLOAD = (HALO * CH + CH // 2, MAIN)
PIX = 144
HID = 256
TROWS = 408
FOLD_REST = COLS + 2 * HALO - MAIN
EARLY = 16
CHUNK = 3
F32, BF16 = jnp.float32, jnp.bfloat16
VMEM = pl.BlockSpec(memory_space=pltpu.VMEM)
HBM = pl.BlockSpec(memory_space=pltpu.HBM)
SMEM = pl.BlockSpec(memory_space=pltpu.SMEM)


def dot_nt(a, b):
    return lax.dot_general(a, b, (((1,), (1,)), ((), ())), preferred_element_type=F32)


def gelu(x):
    inner = x * (0.7978845608028654 + 0.035677408136300125 * (x * x))
    half = 0.5 * x
    return half + half * jnp.tanh(inner)


def cost(us):
    return pl.CostEstimate(flops=int(us * 1e9), bytes_accessed=int(us * 3e6), transcendentals=0)


def call(kernel, ins, operands, outs, scratch, us, mib, out_spec=VMEM, aliases={}):
    return pl.pallas_call(
        kernel,
        out_shape=tuple(jax.ShapeDtypeStruct(shape, F32 if shape == PARTS else BF16) for shape in outs),
        in_specs=ins,
        out_specs=(out_spec,) * len(outs),
        input_output_aliases=aliases,
        scratch_shapes=scratch,
        cost_estimate=cost(us),
        compiler_params=pltpu.CompilerParams(vmem_limit_bytes=mib * 2**20),
    )(*operands)


def masked_row(state_ref, mask_ref, r):
    cover = mask_ref[r].astype(F32)
    row = state_ref[r].astype(F32) * jnp.concatenate([cover] * VARS, axis=0)
    row = jnp.concatenate([row, jnp.zeros((CHANNELS, LANES - COLS), F32)], axis=1)
    return jnp.concatenate([row, jnp.zeros((CH - CHANNELS, LANES), F32)], axis=0)


def tail_out(tail):
    return jnp.concatenate([tail[: CH // 2], tail[CH // 2 :]], axis=1).astype(BF16)


def tail_in(payload_ref):
    low = payload_ref[HALO * CH :, :]
    return jnp.concatenate([low[:, :128], low[:, 128:]], axis=0).astype(F32)


def edge_kernel(state_hbm, mask_hbm, east_ref, west_ref, high_ref, state_ref, mask_ref, sems):
    copies = []
    for i in range(ROWS // CHUNK):
        rows = pl.ds(i * CHUNK, CHUNK)
        for j, (hbm, ref) in enumerate(((mask_hbm, mask_ref), (state_hbm, state_ref))):
            copies.append(pltpu.make_async_copy(hbm.at[rows], ref.at[rows], sems.at[j, i]))
            copies[-1].start()
    low, high = [], []
    for r in range(ROWS):
        if r % CHUNK == 0:
            for copy in copies[2 * (r // CHUNK) : 2 * (r // CHUNK) + 2]:
                copy.wait()
        for held, columns in ((low, slice(0, HALO)), (high, slice(COLS - HALO, COLS))):
            cover = mask_ref[r, :, columns].astype(F32)
            masked = state_ref[r, :, columns].astype(F32) * jnp.concatenate([cover] * VARS, axis=0)
            held.append(jnp.concatenate([masked, jnp.zeros((CH - CHANNELS, HALO), F32)], axis=0))
        k = r - (ROWS - HALO)
        if k >= 0:
            high_ref[k * CH : (k + 1) * CH, :] = masked_row(state_ref, mask_ref, r).astype(BF16)
    rest = [jnp.zeros((CH, 128 - ROWS * HALO), F32)]
    west_ref[...] = jnp.concatenate(low + rest, axis=1).astype(BF16)
    east_ref[...] = jnp.concatenate(high + rest, axis=1).astype(BF16)


def fill_payload(rows_ref, west_ref, east_ref, ref, north):
    lane = lax.broadcasted_iota(jnp.int32, (CH, 128), 1)
    sides = []
    for side, edge_ref in enumerate((west_ref, east_ref)):
        begin = HALO * (REST + side * HALO)
        edge = edge_ref[...].astype(F32)
        rolled = [pltpu.roll(edge, (begin - first * HALO) % 128, 1) for first in (0, ROWS - HALO)]
        inside = jnp.logical_and(lane >= begin, lane < begin + HALO * HALO)
        sides.append(jnp.where(inside, jnp.where(north == 1, rolled[1], rolled[0]), 0.0))
    rest = []
    for k in range(HALO):
        row = rows_ref[(ROWS - HALO) * north + k]
        ref[k * CH : (k + 1) * CH, :] = row[:, :MAIN]
        rest.append(row[:, MAIN:COLS].astype(F32))
    tail = jnp.concatenate(rest + [jnp.zeros((CH, 128 - HALO * REST), F32)], axis=1)
    ref[HALO * CH :, :] = tail_out(tail + sides[0] + sides[1])


def own_rows(rows_ref, west_ref, east_ref, in_ref, packed_ref, f_ref, t_refs, edge_ref):
    edge_ref[0] = flip(west_ref[...].astype(F32))
    edge_ref[1] = flip(east_ref[...].astype(F32))
    for r in range(ROWS):
        t_ref, edge = t_refs.at[r % 2], slice(r * HALO, (r + 1) * HALO)
        t_ref[8 : 8 + LANES, :] = flip(rows_ref[r].astype(F32))
        t_ref[8 - HALO : 8, :] = edge_ref[0, edge, :]
        t_ref[8 + COLS : 8 + COLS + HALO, :] = edge_ref[1, edge, :]
        pack(t_ref, packed_ref, r)
    first_rows(packed_ref, HALO, f_ref, F_FIRST, in_ref, F_FIRST, F_ROWS, straight)


def starts_early():
    lat = lax.axis_index("lat")
    return jnp.logical_and(lax.rem(lat, EARLY) == 0, lat > 0)


def payload_kernel(
    seam_ref, rows_ref, west_ref, east_ref, high_ref, mate_ref, in_ref, pay_ref, kept_ref, packed_ref, f_ref,
    t_refs, edge_ref,
):
    lat, lon = lax.axis_index("lat"), lax.axis_index("lon")
    top = lat == lax.axis_size("lat") - 1

    @pl.when(top)
    def _():
        fill_fold(seam_ref, high_ref, mate_ref, lax.bitwise_xor(lon, 2), pay_ref)
        fill_fold(seam_ref, high_ref, mate_ref, lon, kept_ref)

    @pl.when(jnp.logical_not(top))
    def _():
        fill_payload(rows_ref, west_ref, east_ref, pay_ref, lax.rem(lat, 2))

    @pl.when(starts_early())
    def _():
        own_rows(rows_ref, west_ref, east_ref, in_ref, packed_ref, f_ref, t_refs, edge_ref)


def pack_kernel(
    rows_ref, west_ref, east_ref, in_ref, packed_in, f_in, packed_ref, f_ref, pay_ref, t_refs, edge_ref
):
    fill_payload(rows_ref, west_ref, east_ref, pay_ref, 1 - lax.rem(lax.axis_index("lat"), 2))

    @pl.when(jnp.logical_not(starts_early()))
    def _():
        own_rows(rows_ref, west_ref, east_ref, in_ref, packed_ref, f_ref, t_refs, edge_ref)


def fill_fold(seam_ref, high_ref, mate_ref, target, ref):
    n_lon = lax.axis_size("lon")
    lon = lax.axis_index("lon")
    circle = n_lon * COLS
    held = jnp.concatenate([high_ref[...], mate_ref[...]], axis=1)
    spot = lax.broadcasted_iota(jnp.int32, (2 * LANES, LANES), 0)
    place = spot + jnp.where(spot < LANES, lon * COLS, lax.bitwise_xor(lon, 1) * COLS - LANES)
    column = lax.broadcasted_iota(jnp.int32, (2 * LANES, LANES), 1) - HALO + target * COLS
    source = lax.rem(seam_ref[0] - column + 3 * circle, circle)
    hot = jnp.where(place == source, 1.0, 0.0).astype(BF16)
    rows = jnp.dot(held, hot, preferred_element_type=F32)
    ref[: HALO * CH, :] = rows[:, :MAIN].astype(BF16)
    lane = lax.broadcasted_iota(jnp.int32, (CH, 128), 1)
    tail = jnp.zeros((CH, 128), F32)
    for k in range(HALO):
        shift = FOLD_REST * k
        rolled = pltpu.roll(rows[k * CH : (k + 1) * CH, MAIN:], shift, 1)
        tail += jnp.where(jnp.logical_and(lane >= shift, lane < shift + FOLD_REST), rolled, 0.0)
    ref[HALO * CH :, :] = tail_out(tail)


def ready_kernel(after_ref, state_ref, mask_ref, w_in, w_down, w_mid, w_up, w_out, rows_ref, *padded):
    for r in range(ROWS):
        rows_ref[r] = masked_row(state_ref, mask_ref, r).astype(BF16)
    weight_kernel(w_in, w_down, w_mid, w_up, w_out, *padded)


def weight_kernel(w_in, w_down, w_mid, w_up, w_out, in_ref, down_ref, mid_ref, up_ref, out_ref):
    for ref in (in_ref, down_ref, mid_ref, up_ref, out_ref):
        ref[...] = jnp.zeros(ref.shape, BF16)
    for raw, ref in ((w_in, in_ref), (w_down, down_ref), (w_mid, mid_ref), (w_up, up_ref)):
        for t in range(raw.shape[0]):
            ref[t, : raw.shape[1], :HIDDEN] = raw[t]
    for a in range(3):
        for b in range(3):
            for r in range(3):
                t = 3 * (a + r) + b
                out_ref[r * CH : r * CH + CHANNELS, t * HID : t * HID + HIDDEN] = w_out[3 * a + b]


def flip(block):
    n = block.shape[1]
    return jnp.concatenate([block, jnp.zeros((128 - CH, n), F32)], axis=0).T


def pack(t_ref, a_ref, ai):
    lane = lax.broadcasted_iota(jnp.int32, (PIX, 128), 1)
    odd_left, even, odd, even_right = (t_ref[pl.ds(3 + s, PIX, stride=2), :] for s in range(4))
    even80, odd80 = pltpu.roll(even, CH, 1), pltpu.roll(odd, CH, 1)
    for p, (left, mid, right) in enumerate(((odd_left, even80, odd), (even, odd80, even_right))):
        low = jnp.where(lane < CH, left, mid)
        high = jnp.where(lane < 2 * CH - 128, mid, pltpu.roll(right, 2 * CH - 128, 1))
        a_ref[ai, p * PIX : (p + 1) * PIX, :] = jnp.concatenate([low, high], axis=1).astype(BF16)


def straight(t, n):
    return t


def first_rows(a_ref, begin, f_ref, f_begin, w_ref, fr, n, tap):
    w = []
    for a in range(3):
        w += [w_ref[tap(3 * a + b, 9)] for b in range(3)] + [jnp.zeros((HID - 3 * CH, HID), BF16)]
    w = jnp.concatenate(w, axis=0)
    for q in range(n):
        taps = jnp.concatenate([a_ref[fr + q + a - begin] for a in range(3)], axis=1)
        f_ref[fr + q - f_begin] = gelu(jnp.dot(taps, w, preferred_element_type=F32)).astype(BF16)


def coarse_rows(f_ref, f_begin, c_ref, w_ref, ci, n, tap, held):
    w = jnp.concatenate([w_ref[tap(t, 4)] for t in range(4)], axis=1)
    pieces = []
    for q in range(n):
        piece = [f_ref[2 * (ci + q) + a - f_begin, b * PIX : (b + 1) * PIX, :] for a in range(2) for b in range(2)]
        pieces.append(jnp.concatenate(piece, axis=1))
    coarse = gelu(dot_nt(jnp.concatenate(pieces, axis=0), w))
    if held is not None:
        coarse = coarse * held
    for q in range(n):
        one = coarse[q * PIX : (q + 1) * PIX]
        planes = [pltpu.roll(one, 1, 0), one, pltpu.roll(one, PIX - 1, 0)]
        c_ref[ci + q] = jnp.concatenate(planes, axis=1).astype(BF16)


def mid_rows(c_ref, f_ref, f_begin, j_ref, mid_ref, up_ref, mi, n, tap, held):
    taps = [c_ref[pl.ds(mi + a, n)].reshape(n * PIX, 3 * HID) for a in range(3)]
    w = jnp.concatenate([mid_ref[tap(t, 9)] for t in range(9)], axis=1)
    middle = gelu(dot_nt(jnp.concatenate(taps, axis=1), w)).astype(BF16)
    for a in range(2):
        grown = [dot_nt(middle, up_ref[tap(2 * a + b, 4)]) for b in range(2)]
        for q in range(n):
            row = 2 * (mi + q) + a
            halves = []
            for b in range(2):
                first = f_ref[row + 2 - f_begin, b * PIX : (b + 1) * PIX, :].astype(F32)
                half = gelu(grown[b][q * PIX : (q + 1) * PIX]) + first
                halves.append(half * held if held is not None and q == 0 else half)
            even, odd = halves
            planes = (pltpu.roll(odd, 1, 0), even, odd, pltpu.roll(even, PIX - 1, 0))
            for s, plane in enumerate(planes):
                j_ref[row, s * PIX : (s + 1) * PIX, :] = plane.astype(BF16)


F_FIRST, F_ROWS = 5, 10
C_FIRST, C_ROWS = 3, 4
PACKED = (2 * PIX, HID)
PARTS = (2,) + PACKED
HELD = [pltpu.VMEM((n,) + block, BF16) for n, block in zip((10, 16), ((PIX, 3 * HID), (4 * PIX, HID)))]


def out_taps(j_ref, rows):
    return jnp.concatenate([j_ref[r, b * PIX : (b + 2) * PIX, :] for r in rows for b in range(3)], axis=1)


def inner_kernel(f_ref, down_ref, mid_ref, up_ref, w_out_ref, c_out, part_ref, c_ref, j_ref):
    coarse_rows(f_ref, F_FIRST, c_ref, down_ref, C_FIRST, C_ROWS, straight, None)
    mid_rows(c_ref, f_ref, F_FIRST, j_ref, mid_ref, up_ref, 3, 2, straight, None)
    for i in range(C_ROWS):
        c_out[i] = c_ref[C_FIRST + i]
    part_ref[0] = dot_nt(out_taps(j_ref, (6, 7, 8)), w_out_ref[:, 6 * HID :])
    part_ref[1] = dot_nt(out_taps(j_ref, (7, 8, 9)), w_out_ref[:, : 9 * HID])


def outer_kernel(second, *refs):
    got_ref, refs = refs[0], refs[1:]
    if second:
        half_ref, refs = refs[0], refs[1:]
    else:
        kept_ref, refs = refs[0], refs[1:]
    in_ref, down_ref, mid_ref, up_ref, w_out_ref, state_ref, mask_ref, packed_ref, f_in, c_in, part_ref, next_ref = refs[:12]
    t_refs, edge_ref, a_ref, f_ref, c_ref, j_ref, u_ref = refs[12:19]
    if second:
        out_ref, sems = refs[19:]
    lat = lax.axis_index("lat")
    bottom, top = lat == 0, lat == lax.axis_size("lat") - 1

    def side(north):
        for q in range(2):
            a_ref[5 + 10 * north + q] = packed_ref[10 * north + q]
            c_ref[3 + 2 * north + q] = c_in[2 * north + q]
        for q in range(3):
            f_ref[5 + 7 * north + q] = f_in[7 * north + q]
        edge_ref[0] = flip(tail_in(got_ref))
        t_refs[...] = jnp.zeros(t_refs.shape, F32)
        for k in range(HALO):
            t_ref = t_refs.at[k % 2]
            t_ref[8 : 8 + MAIN, :] = flip(got_ref[k * CH : (k + 1) * CH, :].astype(F32))
            for begin, at, n in ((0, MAIN, REST), (HALO * REST, -HALO, HALO), (HALO * (REST + HALO), COLS, HALO)):
                t_ref[8 + at : 8 + at + n, :] = edge_ref[0, begin + k * n : begin + (k + 1) * n, :]
            pack(t_ref, a_ref, (ROWS + HALO) * north + k)

        if not second and not north:

            @pl.when(bottom)
            def _():
                a_ref[0:HALO] = jnp.zeros((HALO,) + PACKED, BF16)

        if not second and north:
            @pl.when(top)
            def _():
                edge_ref[0] = flip(tail_in(got_ref) + tail_in(kept_ref))
                for k in range(HALO):
                    kk = HALO - 1 - k
                    rows = slice(kk * CH, (kk + 1) * CH)
                    t_ref = t_refs.at[k % 2]
                    t_ref[8 - HALO : 8 - HALO + MAIN, :] = flip(got_ref[rows, :].astype(F32) + kept_ref[rows, :].astype(F32))
                    rest = edge_ref[0, FOLD_REST * kk : FOLD_REST * (kk + 1), :]
                    t_ref[8 - HALO + MAIN : 8 + COLS + HALO, :] = rest
                    pack(t_ref, a_ref, ROWS + HALO + k)

        keep, turn = None, straight
        if not second and north:
            turn = lambda t, n: jnp.where(top, n - 1 - t, t)
        elif not second:
            keep = jnp.where(bottom, 0.0, 1.0).astype(F32)
        first_rows(a_ref, 0, f_ref, 0, in_ref, 4 + 11 * north, 1, straight)
        first_rows(a_ref, 0, f_ref, 0, in_ref, 16 * north, 4, turn)
        coarse_rows(f_ref, 0, c_ref, down_ref, 8 * north, 2, turn, keep)
        coarse_rows(f_ref, 0, c_ref, down_ref, 2 + 5 * north, 1, straight, None)
        mid_rows(c_ref, f_ref, 0, j_ref, mid_ref, up_ref, 5 * north, 3, straight, keep)

        if not second and north:

            @pl.when(top)
            def _():
                mid_rows(c_ref, f_ref, 0, j_ref, mid_ref, up_ref, 7, 1, lambda t, n: n - 1 - t, None)

        if north:
            near = dot_nt(out_taps(j_ref, (10, 11)), w_out_ref[:, 9 * HID :]) + part_ref[1]
            deltas = [near, dot_nt(out_taps(j_ref, range(10, 15)), w_out_ref[...])]
        else:
            near = dot_nt(out_taps(j_ref, (4, 5)), w_out_ref[:, : 6 * HID]) + part_ref[0]
            deltas = [dot_nt(out_taps(j_ref, range(1, 6)), w_out_ref[...]), near]
        copies = []
        if second:
            copies.append(pltpu.make_async_copy(half_ref, next_ref.at[pl.ds(6 * (1 - north), 6)], sems.at[6]))
            copies[0].start()
        for q in range(2):
            flipped = []
            for t in range(2):
                for p in range(2):
                    half = deltas[q][p * PIX : (p + 1) * PIX, t * 128 : (t + 1) * 128]
                    u_ref[pl.ds((2 * q + t) * TROWS + 4 + p, PIX, stride=2), :] = half
                begin = (2 * q + t) * TROWS + 8
                flipped.append(u_ref[begin : begin + LANES, :].T)
            flipped = jnp.concatenate(flipped, axis=0)
            for i in range(3):
                r = 6 * north + 3 * q + i
                delta = flipped[i * CH : i * CH + CHANNELS, :COLS]
                cover = jnp.concatenate([mask_ref[r].astype(F32)] * VARS, axis=0)
                out = ((state_ref[r].astype(F32) + delta) * cover).astype(BF16)
                if second:
                    out_ref[3 * q + i] = out
                    copies.append(pltpu.make_async_copy(out_ref.at[3 * q + i], next_ref.at[r], sems.at[3 * q + i]))
                    copies[-1].start()
                else:
                    next_ref[3 * q + i] = out
        for copy in copies:
            copy.wait()

    for north in range(2):
        pl.when(lax.rem(lat, 2) == (1 - north if second else north))(functools.partial(side, north))


def body(state, sea_mask, seam, w_in, w_down, w_mid, w_up, w_out):
    n_lat, n_lon = lax.axis_size("lat"), lax.axis_size("lon")
    ring = lambda n, d: [(i, (i + d) % n) for i in range(n)]
    state, sea_mask = jnp.swapaxes(state, 0, 1), jnp.swapaxes(sea_mask, 0, 1)
    flat = lambda w: w.reshape((-1,) + w.shape[2:])
    edge = (CH, 128)
    east_going, west_going, high = call(
        edge_kernel, [HBM] * 2, (state, sea_mask), [edge, edge, (HALO * CH, LANES)],
        [
            pltpu.VMEM((ROWS, CHANNELS, COLS), BF16),
            pltpu.VMEM((ROWS, LEVELS, COLS), jnp.int32),
            pltpu.SemaphoreType.DMA((2, ROWS // CHUNK)),
        ],
        1, 60,
    )
    west = lax.ppermute(east_going, "lon", ring(n_lon, 1))
    east = lax.ppermute(west_going, "lon", ring(n_lon, -1))

    axes = ("lat", "lon")
    within = [(i, i ^ 1) for i in range(n_lat * n_lon)]

    def swap(begin):
        pairs = []
        for i in range(n_lat):
            for j in range(n_lon):
                mate = i + 1 if (i - begin) % 2 == 0 else i - 1
                side = i * n_lon + (j ^ (2 if i == n_lat - 1 else 1))
                target = mate * n_lon + j if 0 <= mate < n_lat else side
                pairs.append((i * n_lon + j, target))
        return pairs

    mate = lax.ppermute(high, axes, within)
    rows, *laid = call(
        ready_kernel, [VMEM] * 8,
        (west_going, state, sea_mask, flat(jnp.swapaxes(w_in, 2, 3)), flat(w_down), flat(w_mid), flat(w_up), flat(w_out)),
        [
            (ROWS, CH, LANES),
            (9, CH, HID), (4, HID, HID), (9, HID, HID), (4, HID, HID), (HID, 15 * HID),
        ],
        [], 1.5, 16,
    )
    turning = [pltpu.VMEM((2, TROWS, 128), F32), pltpu.VMEM((2, 128, 128), F32)]
    owned = [(ROWS,) + PACKED, (F_ROWS,) + PACKED]
    pay, kept, packed, f_own = call(
        payload_kernel, [SMEM] + [VMEM] * 6, (seam, rows, west, east, high, mate, laid[0]), [PAYLOAD] * 2 + owned,
        turning, 0.4, 18,
    )
    got = lax.ppermute(pay, axes, swap(1))
    packed, f_own, pay = call(
        pack_kernel, [VMEM] * 6, (rows, west, east, laid[0], packed, f_own), owned + [PAYLOAD], turning, 3.5, 18,
        VMEM, {4: 0, 5: 1},
    )
    got_later = lax.ppermute(pay, axes, swap(0))
    inner = call(
        inner_kernel, [VMEM] * 5, (f_own, *laid[1:]), [(C_ROWS, PIX, 3 * HID), PARTS], HELD, 2.2, 28,
    )
    scratch = turning + [pltpu.VMEM((n,) + PACKED, BF16) for n in (22, 20)] + HELD + [pltpu.VMEM((4 * TROWS, 128), F32)]
    shared = (*laid, state, sea_mask, packed, f_own, *inner)
    (half,) = call(
        functools.partial(outer_kernel, False), [VMEM] * 13, (got, kept, *shared), [(ROWS // 2, CHANNELS, COLS)],
        scratch, 5, 30,
    )
    (out,) = call(
        functools.partial(outer_kernel, True), [VMEM] * 13, (got_later, half, *shared), [(ROWS, CHANNELS, COLS)],
        scratch + [pltpu.VMEM((ROWS // 2, CHANNELS, COLS), BF16), pltpu.SemaphoreType.DMA((ROWS // 2 + 1,))], 6, 30, HBM,
    )
    return jnp.swapaxes(out, 0, 1)


def solution(mesh):
    return jax.shard_map(
        body,
        mesh=mesh,
        in_specs=(P(None, "lat", "lon"), P(None, "lat", "lon"), P(), P(), P(), P(), P(), P()),
        out_specs=P(None, "lat", "lon"),
        check_vma=False,
    )
```

```python
import functools

import jax
import jax.numpy as jnp
from jax import lax
from jax.experimental import pallas as pl
from jax.experimental.pallas import tpu as pltpu
from jax.sharding import PartitionSpec as P

VARS, LEVELS, CHANNELS, HIDDEN = 4, 19, 76, 200
ROWS, COLS = 12, 270
HALO = 5
CH = 80
LANES = 384
MAIN = 256
REST = COLS - MAIN
PAYLOAD = (HALO * CH + CH // 2, MAIN)
PIX = 144
HID = 256
TROWS = 408
FOLD_REST = COLS + 2 * HALO - MAIN
EARLY = 16
CHUNK = 6
F32, BF16 = jnp.float32, jnp.bfloat16
VMEM = pl.BlockSpec(memory_space=pltpu.VMEM)
HBM = pl.BlockSpec(memory_space=pltpu.HBM)
SMEM = pl.BlockSpec(memory_space=pltpu.SMEM)


def dot_nt(a, b):
    return lax.dot_general(a, b, (((1,), (1,)), ((), ())), preferred_element_type=F32)


def gelu(x):
    inner = x * (0.7978845608028654 + 0.035677408136300125 * (x * x))
    half = 0.5 * x
    return half + half * jnp.tanh(inner)


def cost(us):
    return pl.CostEstimate(flops=int(us * 1e9), bytes_accessed=int(us * 3e6), transcendentals=0)


def call(kernel, ins, operands, outs, scratch, us, mib, out_spec=VMEM, aliases={}):
    return pl.pallas_call(
        kernel,
        out_shape=tuple(jax.ShapeDtypeStruct(shape, F32 if shape == PARTS else BF16) for shape in outs),
        in_specs=ins,
        out_specs=(out_spec,) * len(outs),
        input_output_aliases=aliases,
        scratch_shapes=scratch,
        cost_estimate=cost(us),
        compiler_params=pltpu.CompilerParams(vmem_limit_bytes=mib * 2**20),
    )(*operands)


def masked_row(state_ref, mask_ref, r):
    cover = mask_ref[r].astype(F32)
    row = state_ref[r].astype(F32) * jnp.concatenate([cover] * VARS, axis=0)
    row = jnp.concatenate([row, jnp.zeros((CHANNELS, LANES - COLS), F32)], axis=1)
    return jnp.concatenate([row, jnp.zeros((CH - CHANNELS, LANES), F32)], axis=0)


def tail_out(tail):
    return jnp.concatenate([tail[: CH // 2], tail[CH // 2 :]], axis=1).astype(BF16)


def tail_in(payload_ref):
    low = payload_ref[HALO * CH :, :]
    return jnp.concatenate([low[:, :128], low[:, 128:]], axis=0).astype(F32)


def edge_kernel(state_hbm, mask_hbm, east_ref, west_ref, high_ref, state_ref, mask_ref, sems):
    copies = []
    for i in range(ROWS // CHUNK):
        rows = pl.ds(i * CHUNK, CHUNK)
        for j, (hbm, ref) in enumerate(((mask_hbm, mask_ref), (state_hbm, state_ref))):
            copies.append(pltpu.make_async_copy(hbm.at[rows], ref.at[rows], sems.at[j, i]))
            copies[-1].start()
    low, high = [], []
    for r in range(ROWS):
        if r % CHUNK == 0:
            for copy in copies[2 * (r // CHUNK) : 2 * (r // CHUNK) + 2]:
                copy.wait()
        for held, columns in ((low, slice(0, HALO)), (high, slice(COLS - HALO, COLS))):
            cover = mask_ref[r, :, columns].astype(F32)
            masked = state_ref[r, :, columns].astype(F32) * jnp.concatenate([cover] * VARS, axis=0)
            held.append(jnp.concatenate([masked, jnp.zeros((CH - CHANNELS, HALO), F32)], axis=0))
        k = r - (ROWS - HALO)
        if k >= 0:
            high_ref[k * CH : (k + 1) * CH, :] = masked_row(state_ref, mask_ref, r).astype(BF16)
    rest = [jnp.zeros((CH, 128 - ROWS * HALO), F32)]
    west_ref[...] = jnp.concatenate(low + rest, axis=1).astype(BF16)
    east_ref[...] = jnp.concatenate(high + rest, axis=1).astype(BF16)


def fill_payload(rows_ref, west_ref, east_ref, ref, north):
    lane = lax.broadcasted_iota(jnp.int32, (CH, 128), 1)
    sides = []
    for side, edge_ref in enumerate((west_ref, east_ref)):
        begin = HALO * (REST + side * HALO)
        edge = edge_ref[...].astype(F32)
        rolled = [pltpu.roll(edge, (begin - first * HALO) % 128, 1) for first in (0, ROWS - HALO)]
        inside = jnp.logical_and(lane >= begin, lane < begin + HALO * HALO)
        sides.append(jnp.where(inside, jnp.where(north == 1, rolled[1], rolled[0]), 0.0))
    rest = []
    for k in range(HALO):
        row = rows_ref[(ROWS - HALO) * north + k]
        ref[k * CH : (k + 1) * CH, :] = row[:, :MAIN]
        rest.append(row[:, MAIN:COLS].astype(F32))
    tail = jnp.concatenate(rest + [jnp.zeros((CH, 128 - HALO * REST), F32)], axis=1)
    ref[HALO * CH :, :] = tail_out(tail + sides[0] + sides[1])


def own_rows(rows_ref, west_ref, east_ref, in_ref, packed_ref, f_ref, t_refs, edge_ref):
    edge_ref[0] = flip(west_ref[...].astype(F32))
    edge_ref[1] = flip(east_ref[...].astype(F32))
    for r in range(ROWS):
        t_ref, edge = t_refs.at[r % 2], slice(r * HALO, (r + 1) * HALO)
        t_ref[8 : 8 + LANES, :] = flip(rows_ref[r].astype(F32))
        t_ref[8 - HALO : 8, :] = edge_ref[0, edge, :]
        t_ref[8 + COLS : 8 + COLS + HALO, :] = edge_ref[1, edge, :]
        pack(t_ref, packed_ref, r)
    first_rows(Rows(packed_ref, HALO), f_ref, F_FIRST, in_ref, F_FIRST, F_ROWS, straight)


def starts_early():
    lat = lax.axis_index("lat")
    return jnp.logical_and(lax.rem(lat, EARLY) == 0, lat > 0)


def payload_kernel(
    seam_ref, rows_ref, west_ref, east_ref, high_ref, mate_ref, in_ref, pay_ref, kept_ref, packed_ref, f_ref,
    t_refs, edge_ref,
):
    lat, lon = lax.axis_index("lat"), lax.axis_index("lon")
    top = lat == lax.axis_size("lat") - 1

    @pl.when(top)
    def _():
        fill_fold(seam_ref, high_ref, mate_ref, lax.bitwise_xor(lon, 2), pay_ref)
        fill_fold(seam_ref, high_ref, mate_ref, lon, kept_ref)

    @pl.when(jnp.logical_not(top))
    def _():
        fill_payload(rows_ref, west_ref, east_ref, pay_ref, lax.rem(lat, 2))

    @pl.when(starts_early())
    def _():
        own_rows(rows_ref, west_ref, east_ref, in_ref, packed_ref, f_ref, t_refs, edge_ref)


def pack_kernel(
    rows_ref, west_ref, east_ref, in_ref, packed_in, f_in, packed_ref, f_ref, pay_ref, t_refs, edge_ref
):
    fill_payload(rows_ref, west_ref, east_ref, pay_ref, 1 - lax.rem(lax.axis_index("lat"), 2))

    @pl.when(jnp.logical_not(starts_early()))
    def _():
        own_rows(rows_ref, west_ref, east_ref, in_ref, packed_ref, f_ref, t_refs, edge_ref)


def fill_fold(seam_ref, high_ref, mate_ref, target, ref):
    n_lon = lax.axis_size("lon")
    lon = lax.axis_index("lon")
    circle = n_lon * COLS
    held = jnp.concatenate([high_ref[...], mate_ref[...]], axis=1)
    spot = lax.broadcasted_iota(jnp.int32, (2 * LANES, LANES), 0)
    place = spot + jnp.where(spot < LANES, lon * COLS, lax.bitwise_xor(lon, 1) * COLS - LANES)
    column = lax.broadcasted_iota(jnp.int32, (2 * LANES, LANES), 1) - HALO + target * COLS
    source = lax.rem(seam_ref[0] - column + 3 * circle, circle)
    hot = jnp.where(place == source, 1.0, 0.0).astype(BF16)
    rows = jnp.dot(held, hot, preferred_element_type=F32)
    ref[: HALO * CH, :] = rows[:, :MAIN].astype(BF16)
    lane = lax.broadcasted_iota(jnp.int32, (CH, 128), 1)
    tail = jnp.zeros((CH, 128), F32)
    for k in range(HALO):
        shift = FOLD_REST * k
        rolled = pltpu.roll(rows[k * CH : (k + 1) * CH, MAIN:], shift, 1)
        tail += jnp.where(jnp.logical_and(lane >= shift, lane < shift + FOLD_REST), rolled, 0.0)
    ref[HALO * CH :, :] = tail_out(tail)


def ready_kernel(after_ref, state_ref, mask_ref, w_in, w_down, w_mid, w_up, w_out, rows_ref, *padded):
    for r in range(ROWS):
        rows_ref[r] = masked_row(state_ref, mask_ref, r).astype(BF16)
    weight_kernel(w_in, w_down, w_mid, w_up, w_out, *padded)


def weight_kernel(w_in, w_down, w_mid, w_up, w_out, in_ref, down_ref, mid_ref, up_ref, out_ref):
    for ref in (in_ref, down_ref, mid_ref, up_ref, out_ref):
        ref[...] = jnp.zeros(ref.shape, BF16)
    for raw, ref in ((w_in, in_ref), (w_down, down_ref), (w_mid, mid_ref), (w_up, up_ref)):
        for t in range(raw.shape[0]):
            ref[t, : raw.shape[1], :HIDDEN] = raw[t]
    for a in range(3):
        for b in range(3):
            for r in range(3):
                t = 3 * (a + r) + b
                out_ref[r * CH : r * CH + CHANNELS, t * HID : t * HID + HIDDEN] = w_out[3 * a + b]


def flip(block):
    n = block.shape[1]
    return jnp.concatenate([block, jnp.zeros((128 - CH, n), F32)], axis=0).T


def pack(t_ref, a_ref, ai):
    lane = lax.broadcasted_iota(jnp.int32, (PIX, 128), 1)
    odd_left, even, odd, even_right = (t_ref[pl.ds(3 + s, PIX, stride=2), :] for s in range(4))
    even80, odd80 = pltpu.roll(even, CH, 1), pltpu.roll(odd, CH, 1)
    for p, (left, mid, right) in enumerate(((odd_left, even80, odd), (even, odd80, even_right))):
        low = jnp.where(lane < CH, left, mid)
        high = jnp.where(lane < 2 * CH - 128, mid, pltpu.roll(right, 2 * CH - 128, 1))
        a_ref[ai, p * PIX : (p + 1) * PIX, :] = jnp.concatenate([low, high], axis=1).astype(BF16)


def straight(t, n):
    return t


class Rows:
    def __init__(self, own, first, rest=None):
        self.own, self.first, self.rest = own, first, rest
        self.last = first + own.shape[0] - 1

    def __getitem__(self, at):
        row, rest = (at[0], at[1:]) if isinstance(at, tuple) else (at, ())
        if self.first <= row <= self.last:
            return self.own[(row - self.first,) + rest]
        return self.rest[(row,) + rest]


def first_rows(packed, f_ref, f_begin, w_ref, fr, n, tap):
    w = []
    for a in range(3):
        w += [w_ref[tap(3 * a + b, 9)] for b in range(3)] + [jnp.zeros((HID - 3 * CH, HID), BF16)]
    w = jnp.concatenate(w, axis=0)
    for q in range(n):
        taps = jnp.concatenate([packed[fr + q + a] for a in range(3)], axis=1)
        f_ref[fr + q - f_begin] = gelu(jnp.dot(taps, w, preferred_element_type=F32)).astype(BF16)


def coarse_rows(first, c_ref, c_begin, w_ref, ci, n, tap, held):
    w = jnp.concatenate([w_ref[tap(t, 4)] for t in range(4)], axis=1)
    pieces = []
    for q in range(n):
        piece = [first[2 * (ci + q) + a, b * PIX : (b + 1) * PIX, :] for a in range(2) for b in range(2)]
        pieces.append(jnp.concatenate(piece, axis=1))
    coarse = gelu(dot_nt(jnp.concatenate(pieces, axis=0), w))
    if held is not None:
        coarse = coarse * held
    for q in range(n):
        one = coarse[q * PIX : (q + 1) * PIX]
        planes = [pltpu.roll(one, 1, 0), one, pltpu.roll(one, PIX - 1, 0)]
        c_ref[ci + q - c_begin] = jnp.concatenate(planes, axis=1).astype(BF16)


def mid_rows(coarse, first, j_ref, mid_ref, up_ref, mi, n, tap, held, needed):
    taps = [jnp.concatenate([coarse[mi + a + q] for q in range(n)], axis=0) for a in range(3)]
    w = jnp.concatenate([mid_ref[tap(t, 9)] for t in range(9)], axis=1)
    middle = gelu(dot_nt(jnp.concatenate(taps, axis=1), w)).astype(BF16)
    for a in range(2):
        rows = [q for q in range(n) if 2 * (mi + q) + a in needed]
        if not rows:
            continue
        begin, end = rows[0], rows[-1] + 1
        grown = [dot_nt(middle[begin * PIX : end * PIX], up_ref[tap(2 * a + b, 4)]) for b in range(2)]
        for q in rows:
            row = 2 * (mi + q) + a
            halves = []
            for b in range(2):
                skip = first[row + 2, b * PIX : (b + 1) * PIX, :].astype(F32)
                half = gelu(grown[b][(q - begin) * PIX : (q - begin + 1) * PIX]) + skip
                halves.append(half * held if held is not None and q == 0 else half)
            even, odd = halves
            planes = (pltpu.roll(odd, 1, 0), even, odd, pltpu.roll(even, PIX - 1, 0))
            for s, plane in enumerate(planes):
                j_ref[row, s * PIX : (s + 1) * PIX, :] = plane.astype(BF16)


F_FIRST, F_ROWS = 5, 10
C_FIRST, C_ROWS = 3, 4
PACKED = (2 * PIX, HID)
PARTS = (2,) + PACKED
HELD = [pltpu.VMEM((n,) + block, BF16) for n, block in zip((10, 16), ((PIX, 3 * HID), (4 * PIX, HID)))]


def out_taps(j_ref, rows):
    return jnp.concatenate([j_ref[r, b * PIX : (b + 2) * PIX, :] for r in rows for b in range(3)], axis=1)


def inner_kernel(f_ref, down_ref, mid_ref, up_ref, w_out_ref, c_out, part_ref, j_ref):
    first = Rows(f_ref, F_FIRST)
    coarse_rows(first, c_out, C_FIRST, down_ref, C_FIRST, C_ROWS, straight, None)
    mid_rows(Rows(c_out, C_FIRST), first, j_ref, mid_ref, up_ref, 3, 2, straight, None, range(6, 10))
    part_ref[0] = dot_nt(out_taps(j_ref, (6, 7, 8)), w_out_ref[:, 6 * HID :])
    part_ref[1] = dot_nt(out_taps(j_ref, (7, 8, 9)), w_out_ref[:, : 9 * HID])


def outer_kernel(second, *refs):
    got_ref, refs = refs[0], refs[1:]
    if second:
        half_ref, refs = refs[0], refs[1:]
    else:
        kept_ref, refs = refs[0], refs[1:]
    in_ref, down_ref, mid_ref, up_ref, w_out_ref, state_ref, mask_ref, packed_ref, f_in, c_in, part_ref, next_ref = refs[:12]
    t_refs, edge_ref, a_ref, f_ref, c_ref, j_ref, u_ref = refs[12:19]
    if second:
        out_ref, sems = refs[19:]
    lat = lax.axis_index("lat")
    bottom, top = lat == 0, lat == lax.axis_size("lat") - 1

    def side(north):
        packed, first, coarse = Rows(packed_ref, HALO, a_ref), Rows(f_in, F_FIRST, f_ref), Rows(c_in, C_FIRST, c_ref)
        edge_ref[0] = flip(tail_in(got_ref))
        t_refs[...] = jnp.zeros(t_refs.shape, F32)
        for k in range(HALO):
            t_ref = t_refs.at[k % 2]
            t_ref[8 : 8 + MAIN, :] = flip(got_ref[k * CH : (k + 1) * CH, :].astype(F32))
            for begin, at, n in ((0, MAIN, REST), (HALO * REST, -HALO, HALO), (HALO * (REST + HALO), COLS, HALO)):
                t_ref[8 + at : 8 + at + n, :] = edge_ref[0, begin + k * n : begin + (k + 1) * n, :]
            pack(t_ref, a_ref, (ROWS + HALO) * north + k)

        if not second and not north:

            @pl.when(bottom)
            def _():
                a_ref[0:HALO] = jnp.zeros((HALO,) + PACKED, BF16)

        if not second and north:
            @pl.when(top)
            def _():
                edge_ref[0] = flip(tail_in(got_ref) + tail_in(kept_ref))
                for k in range(HALO):
                    kk = HALO - 1 - k
                    rows = slice(kk * CH, (kk + 1) * CH)
                    t_ref = t_refs.at[k % 2]
                    t_ref[8 - HALO : 8 - HALO + MAIN, :] = flip(got_ref[rows, :].astype(F32) + kept_ref[rows, :].astype(F32))
                    rest = edge_ref[0, FOLD_REST * kk : FOLD_REST * (kk + 1), :]
                    t_ref[8 - HALO + MAIN : 8 + COLS + HALO, :] = rest
                    pack(t_ref, a_ref, ROWS + HALO + k)

        keep, turn = None, straight
        if not second and north:
            turn = lambda t, n: jnp.where(top, n - 1 - t, t)
        elif not second:
            keep = jnp.where(bottom, 0.0, 1.0).astype(F32)
        first_rows(packed, f_ref, 0, in_ref, 4 + 11 * north, 1, straight)
        first_rows(packed, f_ref, 0, in_ref, 16 * north, 4, turn)
        coarse_rows(first, c_ref, 0, down_ref, 8 * north, 2, turn, keep)
        coarse_rows(first, c_ref, 0, down_ref, 2 + 5 * north, 1, straight, None)
        mid_rows(coarse, first, j_ref, mid_ref, up_ref, 5 * north, 3, straight, keep, range(1, 15))

        if not second and north:

            @pl.when(top)
            def _():
                mid_rows(coarse, first, j_ref, mid_ref, up_ref, 7, 1, lambda t, n: n - 1 - t, None, (14,))

        if north:
            near = dot_nt(out_taps(j_ref, (10, 11)), w_out_ref[:, 9 * HID :]) + part_ref[1]
            deltas = [near, dot_nt(out_taps(j_ref, range(10, 15)), w_out_ref[...])]
        else:
            near = dot_nt(out_taps(j_ref, (4, 5)), w_out_ref[:, : 6 * HID]) + part_ref[0]
            deltas = [dot_nt(out_taps(j_ref, range(1, 6)), w_out_ref[...]), near]
        copies = []
        if second:
            copies.append(pltpu.make_async_copy(half_ref, next_ref.at[pl.ds(6 * (1 - north), 6)], sems.at[6]))
            copies[0].start()
        for q in range(2):
            flipped = []
            for t in range(2):
                for p in range(2):
                    half = deltas[q][p * PIX : (p + 1) * PIX, t * 128 : (t + 1) * 128]
                    u_ref[pl.ds((2 * q + t) * TROWS + 4 + p, PIX, stride=2), :] = half
                begin = (2 * q + t) * TROWS + 8
                flipped.append(u_ref[begin : begin + LANES, :].T)
            flipped = jnp.concatenate(flipped, axis=0)
            for i in range(3):
                r = 6 * north + 3 * q + i
                delta = flipped[i * CH : i * CH + CHANNELS, :COLS]
                cover = jnp.concatenate([mask_ref[r].astype(F32)] * VARS, axis=0)
                out = ((state_ref[r].astype(F32) + delta) * cover).astype(BF16)
                if second:
                    out_ref[3 * q + i] = out
                    copies.append(pltpu.make_async_copy(out_ref.at[3 * q + i], next_ref.at[r], sems.at[3 * q + i]))
                    copies[-1].start()
                else:
                    next_ref[3 * q + i] = out
        for copy in copies:
            copy.wait()

    for north in range(2):
        pl.when(lax.rem(lat, 2) == (1 - north if second else north))(functools.partial(side, north))


def body(state, sea_mask, seam, w_in, w_down, w_mid, w_up, w_out):
    n_lat, n_lon = lax.axis_size("lat"), lax.axis_size("lon")
    ring = lambda n, d: [(i, (i + d) % n) for i in range(n)]
    state, sea_mask = jnp.swapaxes(state, 0, 1), jnp.swapaxes(sea_mask, 0, 1)
    flat = lambda w: w.reshape((-1,) + w.shape[2:])
    edge = (CH, 128)
    east_going, west_going, high = call(
        edge_kernel, [HBM] * 2, (state, sea_mask), [edge, edge, (HALO * CH, LANES)],
        [
            pltpu.VMEM((ROWS, CHANNELS, COLS), BF16),
            pltpu.VMEM((ROWS, LEVELS, COLS), jnp.int32),
            pltpu.SemaphoreType.DMA((2, ROWS // CHUNK)),
        ],
        1, 60,
    )
    west = lax.ppermute(east_going, "lon", ring(n_lon, 1))
    east = lax.ppermute(west_going, "lon", ring(n_lon, -1))

    axes = ("lat", "lon")
    within = [(i, i ^ 1) for i in range(n_lat * n_lon)]

    def swap(begin):
        pairs = []
        for i in range(n_lat):
            for j in range(n_lon):
                mate = i + 1 if (i - begin) % 2 == 0 else i - 1
                side = i * n_lon + (j ^ (2 if i == n_lat - 1 else 1))
                target = mate * n_lon + j if 0 <= mate < n_lat else side
                pairs.append((i * n_lon + j, target))
        return pairs

    mate = lax.ppermute(high, axes, within)
    rows, *laid = call(
        ready_kernel, [VMEM] * 8,
        (west_going, state, sea_mask, flat(jnp.swapaxes(w_in, 2, 3)), flat(w_down), flat(w_mid), flat(w_up), flat(w_out)),
        [
            (ROWS, CH, LANES),
            (9, CH, HID), (4, HID, HID), (9, HID, HID), (4, HID, HID), (HID, 15 * HID),
        ],
        [], 1.5, 16,
    )
    turning = [pltpu.VMEM((2, TROWS, 128), F32), pltpu.VMEM((2, 128, 128), F32)]
    owned = [(ROWS,) + PACKED, (F_ROWS,) + PACKED]
    pay, kept, packed, f_own = call(
        payload_kernel, [SMEM] + [VMEM] * 6, (seam, rows, west, east, high, mate, laid[0]), [PAYLOAD] * 2 + owned,
        turning, 0.4, 18,
    )
    got = lax.ppermute(pay, axes, swap(1))
    packed, f_own, pay = call(
        pack_kernel, [VMEM] * 6, (rows, west, east, laid[0], packed, f_own), owned + [PAYLOAD], turning, 3.5, 18,
        VMEM, {4: 0, 5: 1},
    )
    got_later = lax.ppermute(pay, axes, swap(0))
    inner = call(
        inner_kernel, [VMEM] * 5, (f_own, *laid[1:]), [(C_ROWS, PIX, 3 * HID), PARTS], HELD[1:], 2.2, 28,
    )
    scratch = turning + [pltpu.VMEM((n,) + PACKED, BF16) for n in (22, 20)] + HELD + [pltpu.VMEM((4 * TROWS, 128), F32)]
    shared = (*laid, state, sea_mask, packed, f_own, *inner)
    (half,) = call(
        functools.partial(outer_kernel, False), [VMEM] * 13, (got, kept, *shared), [(ROWS // 2, CHANNELS, COLS)],
        scratch, 5, 30,
    )
    (out,) = call(
        functools.partial(outer_kernel, True), [VMEM] * 13, (got_later, half, *shared), [(ROWS, CHANNELS, COLS)],
        scratch + [pltpu.VMEM((ROWS // 2, CHANNELS, COLS), BF16), pltpu.SemaphoreType.DMA((ROWS // 2 + 1,))], 6, 30, HBM,
    )
    return jnp.swapaxes(out, 0, 1)


def solution(mesh):
    return jax.shard_map(
        body,
        mesh=mesh,
        in_specs=(P(None, "lat", "lon"), P(None, "lat", "lon"), P(), P(), P(), P(), P(), P()),
        out_specs=P(None, "lat", "lon"),
        check_vma=False,
    )
```

```python
import functools

import jax
import jax.numpy as jnp
from jax import lax
from jax.experimental import pallas as pl
from jax.experimental.pallas import tpu as pltpu
from jax.sharding import PartitionSpec as P

VARS, LEVELS, CHANNELS, HIDDEN = 4, 19, 76, 200
ROWS, COLS = 12, 270
HALO = 5
CH = 80
LANES = 384
MAIN = 256
REST = COLS - MAIN
PAYLOAD = (HALO * CH + CH // 2, MAIN)
PIX = 144
HID = 256
TROWS = 408
FOLD_REST = COLS + 2 * HALO - MAIN
EARLY = 16
CHUNK = 6
F32, BF16 = jnp.float32, jnp.bfloat16
VMEM = pl.BlockSpec(memory_space=pltpu.VMEM)
HBM = pl.BlockSpec(memory_space=pltpu.HBM)
SMEM = pl.BlockSpec(memory_space=pltpu.SMEM)


def dot_nt(a, b):
    return lax.dot_general(a, b, (((1,), (1,)), ((), ())), preferred_element_type=F32)


def gelu(x):
    inner = x * (0.7978845608028654 + 0.035677408136300125 * (x * x))
    half = 0.5 * x
    return half + half * jnp.tanh(inner)


def cost(us):
    return pl.CostEstimate(flops=int(us * 1e9), bytes_accessed=int(us * 3e6), transcendentals=0)


def call(kernel, ins, operands, outs, scratch, us, mib, out_spec=VMEM, aliases={}):
    return pl.pallas_call(
        kernel,
        out_shape=tuple(jax.ShapeDtypeStruct(shape, F32 if shape == PARTS else BF16) for shape in outs),
        in_specs=ins,
        out_specs=(out_spec,) * len(outs),
        input_output_aliases=aliases,
        scratch_shapes=scratch,
        cost_estimate=cost(us),
        compiler_params=pltpu.CompilerParams(vmem_limit_bytes=mib * 2**20),
    )(*operands)


def masked_row(state_ref, mask_ref, r):
    cover = mask_ref[r].astype(F32)
    row = state_ref[r].astype(F32) * jnp.concatenate([cover] * VARS, axis=0)
    row = jnp.concatenate([row, jnp.zeros((CHANNELS, LANES - COLS), F32)], axis=1)
    return jnp.concatenate([row, jnp.zeros((CH - CHANNELS, LANES), F32)], axis=0)


def tail_out(tail):
    return jnp.concatenate([tail[: CH // 2], tail[CH // 2 :]], axis=1).astype(BF16)


def tail_in(payload_ref):
    low = payload_ref[HALO * CH :, :]
    return jnp.concatenate([low[:, :128], low[:, 128:]], axis=0).astype(F32)


def edge_kernel(state_hbm, mask_hbm, east_ref, west_ref, high_ref, state_ref, mask_ref, sems):
    copies = []
    for i in range(ROWS // CHUNK):
        rows = pl.ds(i * CHUNK, CHUNK)
        for j, (hbm, ref) in enumerate(((mask_hbm, mask_ref), (state_hbm, state_ref))):
            copies.append(pltpu.make_async_copy(hbm.at[rows], ref.at[rows], sems.at[j, i]))
            copies[-1].start()
    low, high = [], []
    for r in range(ROWS):
        if r % CHUNK == 0:
            for copy in copies[2 * (r // CHUNK) : 2 * (r // CHUNK) + 2]:
                copy.wait()
        for held, columns in ((low, slice(0, HALO)), (high, slice(COLS - HALO, COLS))):
            cover = mask_ref[r, :, columns].astype(F32)
            masked = state_ref[r, :, columns].astype(F32) * jnp.concatenate([cover] * VARS, axis=0)
            held.append(jnp.concatenate([masked, jnp.zeros((CH - CHANNELS, HALO), F32)], axis=0))
        k = r - (ROWS - HALO)
        if k >= 0:
            high_ref[k * CH : (k + 1) * CH, :] = masked_row(state_ref, mask_ref, r).astype(BF16)
    rest = [jnp.zeros((CH, 128 - ROWS * HALO), F32)]
    west_ref[...] = jnp.concatenate(low + rest, axis=1).astype(BF16)
    east_ref[...] = jnp.concatenate(high + rest, axis=1).astype(BF16)


def fill_payload(rows_ref, west_ref, east_ref, ref, north):
    lane = lax.broadcasted_iota(jnp.int32, (CH, 128), 1)
    sides = []
    for side, edge_ref in enumerate((west_ref, east_ref)):
        begin = HALO * (REST + side * HALO)
        edge = edge_ref[...].astype(F32)
        rolled = [pltpu.roll(edge, (begin - first * HALO) % 128, 1) for first in (0, ROWS - HALO)]
        inside = jnp.logical_and(lane >= begin, lane < begin + HALO * HALO)
        sides.append(jnp.where(inside, jnp.where(north == 1, rolled[1], rolled[0]), 0.0))
    rest = []
    for k in range(HALO):
        row = rows_ref[(ROWS - HALO) * north + k]
        ref[k * CH : (k + 1) * CH, :] = row[:, :MAIN]
        rest.append(row[:, MAIN:COLS].astype(F32))
    tail = jnp.concatenate(rest + [jnp.zeros((CH, 128 - HALO * REST), F32)], axis=1)
    ref[HALO * CH :, :] = tail_out(tail + sides[0] + sides[1])


def own_rows(rows_ref, west_ref, east_ref, in_ref, packed_ref, f_ref, t_refs, edge_ref):
    edge_ref[0] = flip(west_ref[...].astype(F32))
    edge_ref[1] = flip(east_ref[...].astype(F32))
    for r in range(ROWS):
        t_ref, edge = t_refs.at[r % 2], slice(r * HALO, (r + 1) * HALO)
        t_ref[8 : 8 + LANES, :] = flip(rows_ref[r].astype(F32))
        t_ref[8 - HALO : 8, :] = edge_ref[0, edge, :]
        t_ref[8 + COLS : 8 + COLS + HALO, :] = edge_ref[1, edge, :]
        pack(t_ref, packed_ref, r)
    first_rows(Rows(packed_ref, HALO), f_ref, F_FIRST, in_ref, F_FIRST, F_ROWS, straight)


def starts_early():
    lat = lax.axis_index("lat")
    return jnp.logical_and(lax.rem(lat, EARLY) == 0, lat > 0)


def payload_kernel(
    seam_ref, rows_ref, west_ref, east_ref, high_ref, mate_ref, in_ref, pay_ref, kept_ref, packed_ref, f_ref,
    t_refs, edge_ref,
):
    lat, lon = lax.axis_index("lat"), lax.axis_index("lon")
    top = lat == lax.axis_size("lat") - 1

    @pl.when(top)
    def _():
        fill_fold(seam_ref, high_ref, mate_ref, lax.bitwise_xor(lon, 2), pay_ref)
        fill_fold(seam_ref, high_ref, mate_ref, lon, kept_ref)

    @pl.when(jnp.logical_not(top))
    def _():
        fill_payload(rows_ref, west_ref, east_ref, pay_ref, lax.rem(lat, 2))

    @pl.when(starts_early())
    def _():
        own_rows(rows_ref, west_ref, east_ref, in_ref, packed_ref, f_ref, t_refs, edge_ref)


def pack_kernel(
    rows_ref, west_ref, east_ref, in_ref, packed_in, f_in, packed_ref, f_ref, pay_ref, t_refs, edge_ref
):
    fill_payload(rows_ref, west_ref, east_ref, pay_ref, 1 - lax.rem(lax.axis_index("lat"), 2))

    @pl.when(jnp.logical_not(starts_early()))
    def _():
        own_rows(rows_ref, west_ref, east_ref, in_ref, packed_ref, f_ref, t_refs, edge_ref)


def fill_fold(seam_ref, high_ref, mate_ref, target, ref):
    n_lon = lax.axis_size("lon")
    lon = lax.axis_index("lon")
    circle = n_lon * COLS
    held = jnp.concatenate([high_ref[...], mate_ref[...]], axis=1)
    spot = lax.broadcasted_iota(jnp.int32, (2 * LANES, LANES), 0)
    place = spot + jnp.where(spot < LANES, lon * COLS, lax.bitwise_xor(lon, 1) * COLS - LANES)
    column = lax.broadcasted_iota(jnp.int32, (2 * LANES, LANES), 1) - HALO + target * COLS
    source = lax.rem(seam_ref[0] - column + 3 * circle, circle)
    hot = jnp.where(place == source, 1.0, 0.0).astype(BF16)
    rows = jnp.dot(held, hot, preferred_element_type=F32)
    ref[: HALO * CH, :] = rows[:, :MAIN].astype(BF16)
    lane = lax.broadcasted_iota(jnp.int32, (CH, 128), 1)
    tail = jnp.zeros((CH, 128), F32)
    for k in range(HALO):
        shift = FOLD_REST * k
        rolled = pltpu.roll(rows[k * CH : (k + 1) * CH, MAIN:], shift, 1)
        tail += jnp.where(jnp.logical_and(lane >= shift, lane < shift + FOLD_REST), rolled, 0.0)
    ref[HALO * CH :, :] = tail_out(tail)


def ready_kernel(after_ref, state_ref, mask_ref, w_in, w_down, w_mid, w_up, w_out, rows_ref, *padded):
    for r in range(ROWS):
        rows_ref[r] = masked_row(state_ref, mask_ref, r).astype(BF16)
    weight_kernel(w_in, w_down, w_mid, w_up, w_out, *padded)


def weight_kernel(w_in, w_down, w_mid, w_up, w_out, in_ref, down_ref, mid_ref, up_ref, out_ref):
    for ref in (in_ref, down_ref, mid_ref, up_ref, out_ref):
        ref[...] = jnp.zeros(ref.shape, BF16)
    for raw, ref in ((w_in, in_ref), (w_down, down_ref), (w_mid, mid_ref), (w_up, up_ref)):
        for t in range(raw.shape[0]):
            ref[t, : raw.shape[1], :HIDDEN] = raw[t]
    for a in range(3):
        for b in range(3):
            for r in range(3):
                t = 3 * (a + r) + b
                out_ref[r * CH : r * CH + CHANNELS, t * HID : t * HID + HIDDEN] = w_out[3 * a + b]


def flip(block):
    n = block.shape[1]
    return jnp.concatenate([block, jnp.zeros((128 - CH, n), F32)], axis=0).T


def pack(t_ref, a_ref, ai):
    lane = lax.broadcasted_iota(jnp.int32, (PIX, 128), 1)
    odd_left, even, odd, even_right = (t_ref[pl.ds(3 + s, PIX, stride=2), :] for s in range(4))
    even80, odd80 = pltpu.roll(even, CH, 1), pltpu.roll(odd, CH, 1)
    for p, (left, mid, right) in enumerate(((odd_left, even80, odd), (even, odd80, even_right))):
        low = jnp.where(lane < CH, left, mid)
        high = jnp.where(lane < 2 * CH - 128, mid, pltpu.roll(right, 2 * CH - 128, 1))
        a_ref[ai, p * PIX : (p + 1) * PIX, :] = jnp.concatenate([low, high], axis=1).astype(BF16)


def straight(t, n):
    return t


class Rows:
    def __init__(self, own, first, rest=None):
        self.own, self.first, self.rest = own, first, rest
        self.last = first + own.shape[0] - 1

    def __getitem__(self, at):
        row, rest = (at[0], at[1:]) if isinstance(at, tuple) else (at, ())
        if self.first <= row <= self.last:
            return self.own[(row - self.first,) + rest]
        return self.rest[(row,) + rest]


def first_rows(packed, f_ref, f_begin, w_ref, fr, n, tap):
    w = []
    for a in range(3):
        w += [w_ref[tap(3 * a + b, 9)] for b in range(3)] + [jnp.zeros((HID - 3 * CH, HID), BF16)]
    w = jnp.concatenate(w, axis=0)
    for q in range(n):
        for p in (slice(0, PIX), slice(PIX, 2 * PIX)):
            taps = jnp.concatenate([packed[fr + q + a, p, :] for a in range(3)], axis=1)
            f_ref[fr + q - f_begin, p, :] = gelu(jnp.dot(taps, w, preferred_element_type=F32)).astype(BF16)


def coarse_rows(first, c_ref, c_begin, w_ref, ci, n, tap, held):
    w = jnp.concatenate([w_ref[tap(t, 4)] for t in range(4)], axis=1)
    pieces = []
    for q in range(n):
        piece = [first[2 * (ci + q) + a, b * PIX : (b + 1) * PIX, :] for a in range(2) for b in range(2)]
        pieces.append(jnp.concatenate(piece, axis=1))
    coarse = gelu(dot_nt(jnp.concatenate(pieces, axis=0), w))
    if held is not None:
        coarse = coarse * held
    for q in range(n):
        one = coarse[q * PIX : (q + 1) * PIX]
        planes = [pltpu.roll(one, 1, 0), one, pltpu.roll(one, PIX - 1, 0)]
        c_ref[ci + q - c_begin] = jnp.concatenate(planes, axis=1).astype(BF16)


def mid_rows(coarse, first, j_ref, mid_ref, up_ref, mi, n, tap, held, needed):
    taps = [jnp.concatenate([coarse[mi + a + q] for q in range(n)], axis=0) for a in range(3)]
    w = jnp.concatenate([mid_ref[tap(t, 9)] for t in range(9)], axis=1)
    taps = jnp.concatenate(taps, axis=1)
    size = PIX if n == 2 else n * PIX
    middle = [dot_nt(taps[i : i + size], w) for i in range(0, n * PIX, size)]
    middle = gelu(jnp.concatenate(middle, axis=0)).astype(BF16)
    for a in range(2):
        rows = [q for q in range(n) if 2 * (mi + q) + a in needed]
        if not rows:
            continue
        begin, end = rows[0], rows[-1] + 1
        grown = [dot_nt(middle[begin * PIX : end * PIX], up_ref[tap(2 * a + b, 4)]) for b in range(2)]
        for q in rows:
            row = 2 * (mi + q) + a
            halves = []
            for b in range(2):
                skip = first[row + 2, b * PIX : (b + 1) * PIX, :].astype(F32)
                half = gelu(grown[b][(q - begin) * PIX : (q - begin + 1) * PIX]) + skip
                halves.append(half * held if held is not None and q == 0 else half)
            even, odd = halves
            planes = (pltpu.roll(odd, 1, 0), even, odd, pltpu.roll(even, PIX - 1, 0))
            for s, plane in enumerate(planes):
                j_ref[row, s * PIX : (s + 1) * PIX, :] = plane.astype(BF16)


F_FIRST, F_ROWS = 5, 10
C_FIRST, C_ROWS = 3, 4
PACKED = (2 * PIX, HID)
PARTS = (2,) + PACKED
HELD = [pltpu.VMEM((n,) + block, BF16) for n, block in zip((10, 16), ((PIX, 3 * HID), (4 * PIX, HID)))]


def out_taps(j_ref, rows):
    return jnp.concatenate([j_ref[r, b * PIX : (b + 2) * PIX, :] for r in rows for b in range(3)], axis=1)


def inner_kernel(f_ref, down_ref, mid_ref, up_ref, w_out_ref, c_out, part_ref, j_ref):
    first = Rows(f_ref, F_FIRST)
    coarse_rows(first, c_out, C_FIRST, down_ref, C_FIRST, C_ROWS, straight, None)
    mid_rows(Rows(c_out, C_FIRST), first, j_ref, mid_ref, up_ref, 3, 2, straight, None, range(6, 10))
    part_ref[0] = dot_nt(out_taps(j_ref, (6, 7, 8)), w_out_ref[:, 6 * HID :])
    part_ref[1] = dot_nt(out_taps(j_ref, (7, 8, 9)), w_out_ref[:, : 9 * HID])


def outer_kernel(second, *refs):
    got_ref, refs = refs[0], refs[1:]
    if second:
        half_ref, refs = refs[0], refs[1:]
    else:
        kept_ref, refs = refs[0], refs[1:]
    in_ref, down_ref, mid_ref, up_ref, w_out_ref, state_ref, mask_ref, packed_ref, f_in, c_in, part_ref, next_ref = refs[:12]
    t_refs, edge_ref, a_ref, f_ref, c_ref, j_ref, u_ref = refs[12:19]
    if second:
        out_ref, sems = refs[19:]
    lat = lax.axis_index("lat")
    bottom, top = lat == 0, lat == lax.axis_size("lat") - 1

    def side(north):
        packed, first, coarse = Rows(packed_ref, HALO, a_ref), Rows(f_in, F_FIRST, f_ref), Rows(c_in, C_FIRST, c_ref)
        edge_ref[0] = flip(tail_in(got_ref))
        t_refs[...] = jnp.zeros(t_refs.shape, F32)
        for k in range(HALO):
            t_ref = t_refs.at[k % 2]
            t_ref[8 : 8 + MAIN, :] = flip(got_ref[k * CH : (k + 1) * CH, :].astype(F32))
            for begin, at, n in ((0, MAIN, REST), (HALO * REST, -HALO, HALO), (HALO * (REST + HALO), COLS, HALO)):
                t_ref[8 + at : 8 + at + n, :] = edge_ref[0, begin + k * n : begin + (k + 1) * n, :]
            pack(t_ref, a_ref, (ROWS + HALO) * north + k)

        if not second and not north:

            @pl.when(bottom)
            def _():
                a_ref[0:HALO] = jnp.zeros((HALO,) + PACKED, BF16)

        if not second and north:
            @pl.when(top)
            def _():
                edge_ref[0] = flip(tail_in(got_ref) + tail_in(kept_ref))
                for k in range(HALO):
                    kk = HALO - 1 - k
                    rows = slice(kk * CH, (kk + 1) * CH)
                    t_ref = t_refs.at[k % 2]
                    t_ref[8 - HALO : 8 - HALO + MAIN, :] = flip(got_ref[rows, :].astype(F32) + kept_ref[rows, :].astype(F32))
                    rest = edge_ref[0, FOLD_REST * kk : FOLD_REST * (kk + 1), :]
                    t_ref[8 - HALO + MAIN : 8 + COLS + HALO, :] = rest
                    pack(t_ref, a_ref, ROWS + HALO + k)

        keep, turn = None, straight
        if not second and north:
            turn = lambda t, n: jnp.where(top, n - 1 - t, t)
        elif not second:
            keep = jnp.where(bottom, 0.0, 1.0).astype(F32)
        first_rows(packed, f_ref, 0, in_ref, 4 + 11 * north, 1, straight)
        first_rows(packed, f_ref, 0, in_ref, 16 * north, 4, turn)
        coarse_rows(first, c_ref, 0, down_ref, 8 * north, 2, turn, keep)
        coarse_rows(first, c_ref, 0, down_ref, 2 + 5 * north, 1, straight, None)
        mid_rows(coarse, first, j_ref, mid_ref, up_ref, 5 * north, 3, straight, keep, range(1, 15))

        if not second and north:

            @pl.when(top)
            def _():
                mid_rows(coarse, first, j_ref, mid_ref, up_ref, 7, 1, lambda t, n: n - 1 - t, None, (14,))

        if north:
            near = dot_nt(out_taps(j_ref, (10, 11)), w_out_ref[:, 9 * HID :]) + part_ref[1]
            deltas = [near, dot_nt(out_taps(j_ref, range(10, 15)), w_out_ref[...])]
        else:
            near = dot_nt(out_taps(j_ref, (4, 5)), w_out_ref[:, : 6 * HID]) + part_ref[0]
            deltas = [dot_nt(out_taps(j_ref, range(1, 6)), w_out_ref[...]), near]
        copies = []
        if second:
            copies.append(pltpu.make_async_copy(half_ref, next_ref.at[pl.ds(6 * (1 - north), 6)], sems.at[6]))
            copies[0].start()
        for q in range(2):
            flipped = []
            for t in range(2):
                for p in range(2):
                    half = deltas[q][p * PIX : (p + 1) * PIX, t * 128 : (t + 1) * 128]
                    u_ref[pl.ds((2 * q + t) * TROWS + 4 + p, PIX, stride=2), :] = half
                begin = (2 * q + t) * TROWS + 8
                flipped.append(u_ref[begin : begin + LANES, :].T)
            flipped = jnp.concatenate(flipped, axis=0)
            for i in range(3):
                r = 6 * north + 3 * q + i
                delta = flipped[i * CH : i * CH + CHANNELS, :COLS]
                cover = jnp.concatenate([mask_ref[r].astype(F32)] * VARS, axis=0)
                out = ((state_ref[r].astype(F32) + delta) * cover).astype(BF16)
                if second:
                    out_ref[3 * q + i] = out
                    copies.append(pltpu.make_async_copy(out_ref.at[3 * q + i], next_ref.at[r], sems.at[3 * q + i]))
                    copies[-1].start()
                else:
                    next_ref[3 * q + i] = out
        for copy in copies:
            copy.wait()

    for north in range(2):
        pl.when(lax.rem(lat, 2) == (1 - north if second else north))(functools.partial(side, north))


def body(state, sea_mask, seam, w_in, w_down, w_mid, w_up, w_out):
    n_lat, n_lon = lax.axis_size("lat"), lax.axis_size("lon")
    ring = lambda n, d: [(i, (i + d) % n) for i in range(n)]
    state, sea_mask = jnp.swapaxes(state, 0, 1), jnp.swapaxes(sea_mask, 0, 1)
    flat = lambda w: w.reshape((-1,) + w.shape[2:])
    edge = (CH, 128)
    east_going, west_going, high = call(
        edge_kernel, [HBM] * 2, (state, sea_mask), [edge, edge, (HALO * CH, LANES)],
        [
            pltpu.VMEM((ROWS, CHANNELS, COLS), BF16),
            pltpu.VMEM((ROWS, LEVELS, COLS), jnp.int32),
            pltpu.SemaphoreType.DMA((2, ROWS // CHUNK)),
        ],
        1, 60,
    )
    west = lax.ppermute(east_going, "lon", ring(n_lon, 1))
    east = lax.ppermute(west_going, "lon", ring(n_lon, -1))

    axes = ("lat", "lon")
    within = [(i, i ^ 1) for i in range(n_lat * n_lon)]

    def swap(begin):
        pairs = []
        for i in range(n_lat):
            for j in range(n_lon):
                mate = i + 1 if (i - begin) % 2 == 0 else i - 1
                side = i * n_lon + (j ^ (2 if i == n_lat - 1 else 1))
                target = mate * n_lon + j if 0 <= mate < n_lat else side
                pairs.append((i * n_lon + j, target))
        return pairs

    mate = lax.ppermute(high, axes, within)
    rows, *laid = call(
        ready_kernel, [VMEM] * 8,
        (west_going, state, sea_mask, flat(jnp.swapaxes(w_in, 2, 3)), flat(w_down), flat(w_mid), flat(w_up), flat(w_out)),
        [
            (ROWS, CH, LANES),
            (9, CH, HID), (4, HID, HID), (9, HID, HID), (4, HID, HID), (HID, 15 * HID),
        ],
        [], 1.5, 16,
    )
    turning = [pltpu.VMEM((2, TROWS, 128), F32), pltpu.VMEM((2, 128, 128), F32)]
    owned = [(ROWS,) + PACKED, (F_ROWS,) + PACKED]
    pay, kept, packed, f_own = call(
        payload_kernel, [SMEM] + [VMEM] * 6, (seam, rows, west, east, high, mate, laid[0]), [PAYLOAD] * 2 + owned,
        turning, 0.4, 18,
    )
    got = lax.ppermute(pay, axes, swap(1))
    packed, f_own, pay = call(
        pack_kernel, [VMEM] * 6, (rows, west, east, laid[0], packed, f_own), owned + [PAYLOAD], turning, 3.5, 18,
        VMEM, {4: 0, 5: 1},
    )
    got_later = lax.ppermute(pay, axes, swap(0))
    inner = call(
        inner_kernel, [VMEM] * 5, (f_own, *laid[1:]), [(C_ROWS, PIX, 3 * HID), PARTS], HELD[1:], 2.2, 28,
    )
    scratch = turning + [pltpu.VMEM((n,) + PACKED, BF16) for n in (22, 20)] + HELD + [pltpu.VMEM((4 * TROWS, 128), F32)]
    shared = (*laid, state, sea_mask, packed, f_own, *inner)
    (half,) = call(
        functools.partial(outer_kernel, False), [VMEM] * 13, (got, kept, *shared), [(ROWS // 2, CHANNELS, COLS)],
        scratch, 5, 30,
    )
    (out,) = call(
        functools.partial(outer_kernel, True), [VMEM] * 13, (got_later, half, *shared), [(ROWS, CHANNELS, COLS)],
        scratch + [pltpu.VMEM((ROWS // 2, CHANNELS, COLS), BF16), pltpu.SemaphoreType.DMA((ROWS // 2 + 1,))], 6, 30, HBM,
    )
    return jnp.swapaxes(out, 0, 1)


def solution(mesh):
    return jax.shard_map(
        body,
        mesh=mesh,
        in_specs=(P(None, "lat", "lon"), P(None, "lat", "lon"), P(), P(), P(), P(), P(), P()),
        out_specs=P(None, "lat", "lon"),
        check_vma=False,
    )
```
